768 devices in a mesh: grp: 64 (over y, z_hi, core), dom: 12 (over x, z_lo).
Axes of the slice: x: 4, y: 8, z: 12 (z_hi: 4, z_lo: 3; z = z_hi * 3 + z_lo), core: 2. Of those that a mesh axis runs over, the one named last changes fastest.
Arguments:
- grids: float32 [128, 8, 64, 1536], P('grp', None, None, 'dom'), may hold values from -6 to 6
- table: int32 [128, 8], P('grp'), may hold values from 0 to 63, all different within a row
- coefs: int32 [128], P('grp'), may hold values from -10 to 10, as said below
Outputs:
- combined: float32 [128, 8, 64, 1536], P('grp', None, None, 'dom')
The draws below stay inside these ranges and needn't reach their ends.
Inputs may be any that keep to these rules, and one draw needn't show every extreme that they name: The 8 entries of a row of table differ, and every subspace is named by some row. `coefs`: every coefficient is one of 1, -5, 10, -10, 5, -1.
All inputs are finite; a program needn't handle non-finite values.
Results may differ from the reference program's by a relative error of at most 0.00007.
Values sent between devices are 32-bit elements; how exact they have to be, the bound alone decides.
No kernel may reach another device: no remote copies, remote signals or barrier semaphores. Data moves between devices by JAX's collectives and lax.ppermute only.
A program may use at most 32 MiB of HBM per device.

```python
import jax
import jax.numpy as jnp
from jax import lax

FIELDS = 64
SLOTS = 8
GRIDS = 128
SUBS = 64
POINTS = 1536


def draw_coefs(key, part):
    picks = jax.random.randint(jax.random.fold_in(key, 17), (GRIDS,), 0, 6)
    values = jnp.array([1, -5, 10, -10, 5, -1], dtype=jnp.int32)
    return values[picks].astype(jnp.int32)


def shard_levels(key, extent, pieces, smallest, largest):
    def one(axis_at, parts):
        heights = jax.random.uniform(jax.random.fold_in(jax.random.fold_in(key, 6), axis_at), (parts,), jnp.float32, smallest / len(pieces), largest / len(pieces))
        return jnp.repeat(jnp.exp(heights), extent[axis_at] // parts).reshape((-1,) + (1,) * (len(extent) - axis_at - 1))

    factor_of = one(*pieces[0])
    for cut in pieces[1:]:
        factor_of = factor_of * one(*cut)
    return factor_of


def choose_distinct(rng, rows, number_of, top, lift):
    order = jax.random.permutation(jax.random.fold_in(rng, 1), number_of)
    boost = order
    for power in range(3):
        boost = boost * boost // number_of
    boost = boost * lift // number_of
    tickets = jax.random.randint(jax.random.fold_in(rng, 2), (rows, number_of), 0, 4096) + boost
    fixed_rows = jax.random.permutation(jax.random.fold_in(rng, 3), rows)[jnp.arange(number_of) % rows]
    tickets = jnp.where(jnp.arange(rows)[:, None] == fixed_rows[None, :], 1 << 14, tickets)
    score = tickets * number_of + jnp.arange(number_of)
    return lax.top_k(score.astype(jnp.int32), top)[1].astype(jnp.int32)


def scatter_about(own_key, extent, width, bound, cuts=(), kind=jnp.bfloat16):
    factor_of = shard_levels(own_key, extent, cuts, -0.22, 0.18) if cuts else 1.0
    result = jax.random.normal(own_key, extent, jnp.float32) * width * factor_of
    return jnp.minimum(jnp.maximum(result, -bound), bound).astype(kind)


def setup_inputs(seed: int = 0) -> dict:
    splits = jax.random.split(jax.random.key(seed), 4)
    grids = scatter_about(splits[0], (GRIDS, SLOTS, FIELDS, POINTS), 1.0, 6.0, ((0, 64), (3, 12)), jnp.float32)
    table = choose_distinct(splits[1], GRIDS, SUBS, SLOTS, 0)
    coefs = draw_coefs(jax.random.fold_in(splits[3], 71), 0)
    return dict(grids=grids, table=table, coefs=coefs)


def reference(grids, table, coefs):
    count = GRIDS * SLOTS
    data = grids.reshape(count, FIELDS * POINTS)
    weight = jnp.repeat(coefs.astype(jnp.float32), SLOTS)
    labels = table.reshape(count).astype(jnp.int32)
    sparse = jax.ops.segment_sum(data * weight[:, None], labels, num_segments=SUBS)
    combined = sparse[labels]
    return combined.reshape(GRIDS, SLOTS, FIELDS, POINTS)
```

```python
import jax
import jax.numpy as jnp
from jax import lax
from jax.sharding import PartitionSpec as P

SUBS = 64


def on_device(grids, table, coefs):
    local_grids, slots, fields, points = grids.shape
    count = local_grids * slots
    size = lax.axis_size("grp")
    rows = fields // size
    known = jnp.concatenate([table.reshape(count), jnp.repeat(coefs, slots)])
    known = lax.all_gather(known, "grp").reshape(size, 2, count)
    labels = known[:, 0].reshape(size * count)
    weight = known[:, 1].reshape(size * count).astype(jnp.float32)
    sent = grids.reshape(count, size, rows, points).transpose(1, 0, 2, 3)
    parts = lax.all_to_all(sent, "grp", 0, 0, tiled=True)
    parts = parts.reshape(size * count, rows * points)
    wanted = jnp.arange(SUBS, dtype=jnp.int32)
    onehot = (labels[None, :] == wanted[:, None]).astype(jnp.float32)
    sparse = jnp.dot(
        onehot * weight[None, :],
        parts,
        precision=lax.Precision.HIGHEST,
        preferred_element_type=jnp.float32,
    )
    picks = jnp.dot(
        onehot.T, sparse, precision=lax.Precision.HIGHEST, preferred_element_type=jnp.float32
    )
    back = lax.all_to_all(picks.reshape(size, count, rows, points), "grp", 0, 0, tiled=True)
    return back.transpose(1, 0, 2, 3).reshape(local_grids, slots, fields, points)


def solution(mesh):
    return jax.shard_map(
        on_device,
        mesh=mesh,
        in_specs=(P("grp", None, None, "dom"), P("grp", None), P("grp")),
        out_specs=P("grp", None, None, "dom"),
        check_vma=False,
    )
```

```python
import jax
import jax.numpy as jnp
from jax import lax
from jax.sharding import PartitionSpec as P

SUBS = 64
Y, Z, CORES = 8, 4, 2
PLANES = [[(y * Z + z) * CORES + c for y in range(Y) for c in range(CORES)] for z in range(Z)]
COLUMNS = [[(y * Z + z) * CORES + c for z in range(Z)] for y in range(Y) for c in range(CORES)]
TILE = 8


def exchange(value):
    return lax.all_to_all(value, "grp", 0, 0, tiled=True, axis_index_groups=PLANES)


def on_device(grids, table, coefs):
    local_grids, slots, fields, points = grids.shape
    count = local_grids * slots
    peers = Y * CORES
    own = fields // peers
    blocks = grids.reshape(count, peers, own, points).transpose(1, 2, 0, 3)
    blocks = blocks.reshape(peers, own * count, points)
    known = jnp.stack([table.reshape(count), jnp.repeat(coefs, slots)]).astype(jnp.float32)
    known = jnp.pad(known, ((0, TILE - 2), (0, points - count)))
    known = jnp.broadcast_to(known[None], (peers, TILE, points))
    got = exchange(jnp.concatenate([blocks, known], axis=1))
    labels = got[:, own * count, :count].reshape(peers * count).astype(jnp.int32)
    weight = got[:, own * count + 1, :count].reshape(peers * count)
    parts = got[:, : own * count].reshape(peers, own, count, points)
    wanted = jnp.arange(SUBS, dtype=jnp.int32)
    onehot = (labels[None, :] == wanted[:, None]).astype(jnp.float32)
    weighted = onehot * weight[None, :]
    partial = jnp.stack(
        [
            jnp.dot(
                weighted,
                parts[:, j].reshape(peers * count, points),
                precision=lax.Precision.HIGHEST,
                preferred_element_type=jnp.float32,
            )
            for j in range(own)
        ]
    )
    sparse = jnp.sum(lax.all_gather(partial, "grp", axis_index_groups=COLUMNS), axis=0)
    picks = jnp.stack(
        [
            jnp.dot(
                onehot.T,
                sparse[j],
                precision=lax.Precision.HIGHEST,
                preferred_element_type=jnp.float32,
            ).reshape(peers, count, points)
            for j in range(own)
        ],
        axis=1,
    )
    back = exchange(picks.reshape(peers, own * count, points))
    back = back.reshape(fields, count, points).transpose(1, 0, 2)
    return back.reshape(local_grids, slots, fields, points)


def solution(mesh):
    return jax.shard_map(
        on_device,
        mesh=mesh,
        in_specs=(P("grp", None, None, "dom"), P("grp", None), P("grp")),
        out_specs=P("grp", None, None, "dom"),
        check_vma=False,
    )
```

```python
import jax
import jax.numpy as jnp
from jax import lax
from jax.experimental import pallas as pl
from jax.experimental.pallas import tpu as pltpu
from jax.sharding import PartitionSpec as P

SUBS = 64
Y, Z, CORES = 8, 4, 2
PLANES = [[(y * Z + z) * CORES + c for y in range(Y) for c in range(CORES)] for z in range(Z)]
COLUMNS = [[(y * Z + z) * CORES + c for z in range(Z)] for y in range(Y) for c in range(CORES)]
PEERS = Y * CORES
COUNT = 16
FIELDS = 64
POINTS = 128
OWN = FIELDS // PEERS
ROWS = OWN * COUNT
TILE = 8
VMEM = pl.BlockSpec(memory_space=pltpu.VMEM)
ROOM = pltpu.CompilerParams(vmem_limit_bytes=8 << 20)
SMEM = pl.BlockSpec(memory_space=pltpu.SMEM)


def exchange(value):
    return lax.all_to_all(value, "grp", 0, 0, tiled=True, axis_index_groups=PLANES)


def thirds(value):
    high = value.astype(jnp.bfloat16)
    rest = value - high.astype(jnp.float32)
    mid = rest.astype(jnp.bfloat16)
    low = (rest - mid.astype(jnp.float32)).astype(jnp.bfloat16)
    return high, mid, low


def pack_kernel(table_ref, coefs_ref, grids_ref, out_ref):
    slots = table_ref.shape[1]
    lane = lax.broadcasted_iota(jnp.int32, (TILE, POINTS), 1) % COUNT
    row = lax.broadcasted_iota(jnp.int32, (TILE, POINTS), 0)
    known = jnp.zeros((TILE, POINTS), jnp.int32)
    for i in range(COUNT):
        g, k = divmod(i, slots)
        known = jnp.where(lane == i, jnp.where(row == 0, table_ref[g, k], coefs_ref[g]), known)
    known = known.astype(jnp.float32)
    for peer in range(PEERS):
        for j in range(OWN):
            out_ref[peer, j * COUNT : (j + 1) * COUNT, :] = grids_ref[:, peer * OWN + j, :]
        out_ref[peer, ROWS:, :] = known


def in_one_row(rows):
    peer = lax.broadcasted_iota(jnp.int32, rows.shape, 0)
    part = lax.broadcasted_iota(jnp.int32, rows.shape, 1) // COUNT
    per = POINTS // COUNT
    return jnp.concatenate(
        [
            jnp.sum(jnp.where(peer == part + h * per, rows, 0.0), axis=0, keepdims=True)
            for h in range(PEERS // per)
        ],
        axis=1,
    )


def sum_kernel(got_ref, out_ref, labels_ref):
    labels = in_one_row(got_ref[:, ROWS, :])
    weight = in_one_row(got_ref[:, ROWS + 1, :])
    wanted = lax.broadcasted_iota(jnp.int32, (SUBS, PEERS * COUNT), 0).astype(jnp.float32)
    weighted = jnp.where(labels == wanted, weight, 0.0).astype(jnp.bfloat16)
    data = jnp.concatenate(
        [
            got_ref[:, j * COUNT : (j + 1) * COUNT, :].reshape(PEERS * COUNT, POINTS)
            for j in range(OWN)
        ],
        axis=1,
    )
    high, mid, low = (
        jnp.dot(weighted, part, preferred_element_type=jnp.float32) for part in thirds(data)
    )
    total = high + (mid + low)
    for j in range(OWN):
        out_ref[j] = total[:, j * POINTS : (j + 1) * POINTS]
    labels_ref[...] = jnp.broadcast_to(labels, labels_ref.shape)


def pick_kernel(every_ref, labels_ref, out_ref):
    sparse = jnp.concatenate(
        [
            (every_ref[0, j] + every_ref[1, j]) + (every_ref[2, j] + every_ref[3, j])
            for j in range(OWN)
        ],
        axis=1,
    )
    wanted = lax.broadcasted_iota(jnp.int32, (SUBS, PEERS * COUNT), 0).astype(jnp.float32)
    onehot = (labels_ref[0:1, :] == wanted).astype(jnp.float32).T.astype(jnp.bfloat16)
    picks = jnp.dot(
        jnp.concatenate([onehot] * 3, axis=1),
        jnp.concatenate(thirds(sparse), axis=0),
        preferred_element_type=jnp.float32,
    )
    for j in range(OWN):
        out_ref[:, j * COUNT : (j + 1) * COUNT, :] = picks[
            :, j * POINTS : (j + 1) * POINTS
        ].reshape(PEERS, COUNT, POINTS)


def unpack_kernel(back_ref, out_ref):
    for r in range(COUNT):
        for f in range(0, FIELDS, TILE):
            out_ref[r, f : f + TILE, :] = back_ref[f : f + TILE, r, :]


def on_device(grids, table, coefs):
    f32 = jnp.float32
    message = pl.pallas_call(
        pack_kernel,
        out_shape=jax.ShapeDtypeStruct((PEERS, ROWS + TILE, POINTS), f32),
        in_specs=[SMEM, SMEM, VMEM],
        out_specs=VMEM,
        compiler_params=ROOM,
    )(table, coefs, grids.reshape(COUNT, FIELDS, POINTS))
    partial, labels = pl.pallas_call(
        sum_kernel,
        out_shape=(
            jax.ShapeDtypeStruct((OWN, SUBS, POINTS), f32),
            jax.ShapeDtypeStruct((TILE, PEERS * COUNT), f32),
        ),
        in_specs=[VMEM],
        out_specs=(VMEM, VMEM),
        compiler_params=ROOM,
    )(exchange(message))
    every = lax.all_gather(partial, "grp", axis_index_groups=COLUMNS)
    picks = pl.pallas_call(
        pick_kernel,
        out_shape=jax.ShapeDtypeStruct((PEERS, ROWS, POINTS), f32),
        in_specs=[VMEM, VMEM],
        out_specs=VMEM,
        compiler_params=ROOM,
    )(every, labels)
    back = exchange(picks).reshape(FIELDS, COUNT, POINTS)
    combined = pl.pallas_call(
        unpack_kernel,
        out_shape=jax.ShapeDtypeStruct((COUNT, FIELDS, POINTS), f32),
        in_specs=[VMEM],
        out_specs=VMEM,
        compiler_params=ROOM,
    )(back)
    return combined.reshape(grids.shape)


def solution(mesh):
    return jax.shard_map(
        on_device,
        mesh=mesh,
        in_specs=(P("grp", None, None, "dom"), P("grp", None), P("grp")),
        out_specs=P("grp", None, None, "dom"),
        check_vma=False,
    )
```

```python
import jax
import jax.numpy as jnp
from jax import lax
from jax.experimental import pallas as pl
from jax.experimental.pallas import tpu as pltpu
from jax.sharding import PartitionSpec as P

SUBS = 64
Y, Z, CORES = 8, 4, 2
PLANES = [[(y * Z + z) * CORES + c for y in range(Y) for c in range(CORES)] for z in range(Z)]
COLUMNS = [[(y * Z + z) * CORES + c for z in range(Z)] for y in range(Y) for c in range(CORES)]
PEERS = Y * CORES
COUNT = 16
FIELDS = 64
POINTS = 128
OWN = FIELDS // PEERS
ROWS = OWN * COUNT
TILE = 8
CHUNKS = 4
VMEM = pl.BlockSpec(memory_space=pltpu.VMEM)
ROOM = pltpu.CompilerParams(vmem_limit_bytes=8 << 20)
HBM = pl.BlockSpec(memory_space=pltpu.HBM)


def exchange(value):
    return lax.all_to_all(value, "grp", 0, 0, tiled=True, axis_index_groups=PLANES)


def in_hbm(value):
    return pltpu.with_memory_space_constraint(value, pltpu.HBM)


def thirds(value):
    high = value.astype(jnp.bfloat16)
    rest = value - high.astype(jnp.float32)
    mid = rest.astype(jnp.bfloat16)
    low = (rest - mid.astype(jnp.float32)).astype(jnp.bfloat16)
    return high, mid, low


def pack_kernel(table_hbm, coefs_hbm, grids_hbm, out_ref, table, coefs, grids, known_sem, grids_sem):
    known_copies = [
        pltpu.make_async_copy(table_hbm, table, known_sem.at[0]),
        pltpu.make_async_copy(coefs_hbm, coefs, known_sem.at[1]),
    ]
    chunk = FIELDS // CHUNKS
    spans = [pl.ds(i * chunk, chunk) for i in range(CHUNKS)]
    copies = [
        pltpu.make_async_copy(grids_hbm.at[:, span, :], grids.at[:, span, :], grids_sem.at[i])
        for i, span in enumerate(spans)
    ]
    for copy in known_copies + copies:
        copy.start()
    for copy in known_copies:
        copy.wait()
    slots = table.shape[1]
    lane = lax.broadcasted_iota(jnp.int32, (TILE, POINTS), 1) % COUNT
    row = lax.broadcasted_iota(jnp.int32, (TILE, POINTS), 0)
    known = jnp.zeros((TILE, POINTS), jnp.int32)
    for i in range(COUNT):
        g, k = divmod(i, slots)
        known = jnp.where(lane == i, jnp.where(row == 0, table[g, k], coefs[g]), known)
    known = known.astype(jnp.float32)
    for peer in range(PEERS):
        out_ref[peer, ROWS:, :] = known
    for i, copy in enumerate(copies):
        copy.wait()
        for f in range(i * chunk, (i + 1) * chunk):
            peer, j = divmod(f, OWN)
            out_ref[peer, j * COUNT : (j + 1) * COUNT, :] = grids[:, f, :]


def in_one_row(rows):
    peer = lax.broadcasted_iota(jnp.int32, rows.shape, 0)
    part = lax.broadcasted_iota(jnp.int32, rows.shape, 1) // COUNT
    per = POINTS // COUNT
    return jnp.concatenate(
        [
            jnp.sum(jnp.where(peer == part + h * per, rows, 0.0), axis=0, keepdims=True)
            for h in range(PEERS // per)
        ],
        axis=1,
    )


def sum_kernel(got_ref, out_ref, labels_ref):
    labels = in_one_row(got_ref[:, ROWS, :])
    weight = in_one_row(got_ref[:, ROWS + 1, :])
    wanted = lax.broadcasted_iota(jnp.int32, (SUBS, PEERS * COUNT), 0).astype(jnp.float32)
    weighted = jnp.where(labels == wanted, weight, 0.0).astype(jnp.bfloat16)
    data = jnp.concatenate(
        [
            got_ref[:, j * COUNT : (j + 1) * COUNT, :].reshape(PEERS * COUNT, POINTS)
            for j in range(OWN)
        ],
        axis=1,
    )
    high, mid, low = (
        jnp.dot(weighted, part, preferred_element_type=jnp.float32) for part in thirds(data)
    )
    total = high + (mid + low)
    for j in range(OWN):
        out_ref[j] = total[:, j * POINTS : (j + 1) * POINTS]
    labels_ref[...] = jnp.broadcast_to(labels, labels_ref.shape)


def pick_kernel(every_ref, labels_ref, out_ref):
    sparse = jnp.concatenate(
        [
            (every_ref[0, j] + every_ref[1, j]) + (every_ref[2, j] + every_ref[3, j])
            for j in range(OWN)
        ],
        axis=1,
    )
    wanted = lax.broadcasted_iota(jnp.int32, (SUBS, PEERS * COUNT), 0).astype(jnp.float32)
    onehot = (labels_ref[0:1, :] == wanted).astype(jnp.float32).T.astype(jnp.bfloat16)
    picks = jnp.dot(
        jnp.concatenate([onehot] * 3, axis=1),
        jnp.concatenate(thirds(sparse), axis=0),
        preferred_element_type=jnp.float32,
    )
    for j in range(OWN):
        out_ref[:, j * COUNT : (j + 1) * COUNT, :] = picks[
            :, j * POINTS : (j + 1) * POINTS
        ].reshape(PEERS, COUNT, POINTS)


def unpack_kernel(back_ref, out_hbm, held, sem):
    chunk = COUNT // CHUNKS
    copies = []
    for i in range(CHUNKS):
        for r in range(i * chunk, (i + 1) * chunk):
            for f in range(0, FIELDS, TILE):
                held[r, f : f + TILE, :] = back_ref[f : f + TILE, r, :]
        span = pl.ds(i * chunk, chunk)
        copies.append(pltpu.make_async_copy(held.at[span], out_hbm.at[span], sem.at[i]))
        copies[-1].start()
    for copy in copies:
        copy.wait()


def on_device(grids, table, coefs):
    f32 = jnp.float32
    message = pl.pallas_call(
        pack_kernel,
        out_shape=jax.ShapeDtypeStruct((PEERS, ROWS + TILE, POINTS), f32),
        in_specs=[HBM, HBM, HBM],
        out_specs=VMEM,
        scratch_shapes=[
            pltpu.SMEM(table.shape, table.dtype),
            pltpu.SMEM(coefs.shape, coefs.dtype),
            pltpu.VMEM((COUNT, FIELDS, POINTS), f32),
            pltpu.SemaphoreType.DMA((2,)),
            pltpu.SemaphoreType.DMA((CHUNKS,)),
        ],
        compiler_params=ROOM,
    )(*map(in_hbm, (table, coefs, grids.reshape(COUNT, FIELDS, POINTS))))
    partial, labels = pl.pallas_call(
        sum_kernel,
        out_shape=(
            jax.ShapeDtypeStruct((OWN, SUBS, POINTS), f32),
            jax.ShapeDtypeStruct((TILE, PEERS * COUNT), f32),
        ),
        in_specs=[VMEM],
        out_specs=(VMEM, VMEM),
        compiler_params=ROOM,
    )(exchange(message))
    every = lax.all_gather(partial, "grp", axis_index_groups=COLUMNS)
    picks = pl.pallas_call(
        pick_kernel,
        out_shape=jax.ShapeDtypeStruct((PEERS, ROWS, POINTS), f32),
        in_specs=[VMEM, VMEM],
        out_specs=VMEM,
        compiler_params=ROOM,
    )(every, labels)
    back = exchange(picks).reshape(FIELDS, COUNT, POINTS)
    combined = pl.pallas_call(
        unpack_kernel,
        out_shape=jax.ShapeDtypeStruct((COUNT, FIELDS, POINTS), f32),
        in_specs=[VMEM],
        out_specs=HBM,
        scratch_shapes=[
            pltpu.VMEM((COUNT, FIELDS, POINTS), f32),
            pltpu.SemaphoreType.DMA((CHUNKS,)),
        ],
        compiler_params=ROOM,
    )(back)
    return combined.reshape(grids.shape)


def solution(mesh):
    return jax.shard_map(
        on_device,
        mesh=mesh,
        in_specs=(P("grp", None, None, "dom"), P("grp", None), P("grp")),
        out_specs=P("grp", None, None, "dom"),
        check_vma=False,
    )
```

```python
import jax
import jax.numpy as jnp
from jax import lax
from jax.experimental import pallas as pl
from jax.experimental.pallas import tpu as pltpu
from jax.sharding import PartitionSpec as P

SUBS = 64
COUNT = 16
FIELDS = 64
POINTS = 128
PEERS = 64
ROWS = COUNT + 1
TILE = 8
CHUNKS = 4
VMEM = pl.BlockSpec(memory_space=pltpu.VMEM)
ROOM = pltpu.CompilerParams(vmem_limit_bytes=8 << 20)
HBM = pl.BlockSpec(memory_space=pltpu.HBM)


def in_hbm(value):
    return pltpu.with_memory_space_constraint(value, pltpu.HBM)


def thirds(value):
    high = value.astype(jnp.bfloat16)
    rest = value - high.astype(jnp.float32)
    mid = rest.astype(jnp.bfloat16)
    low = (rest - mid.astype(jnp.float32)).astype(jnp.bfloat16)
    return high, mid, low


def pack_kernel(table_hbm, coefs_hbm, grids_hbm, out_ref, table, coefs, grids, known_sem, grids_sem):
    known_copies = [
        pltpu.make_async_copy(table_hbm, table, known_sem.at[0]),
        pltpu.make_async_copy(coefs_hbm, coefs, known_sem.at[1]),
    ]
    chunk = FIELDS // CHUNKS
    spans = [pl.ds(i * chunk, chunk) for i in range(CHUNKS)]
    copies = [
        pltpu.make_async_copy(grids_hbm.at[:, span, :], grids.at[:, span, :], grids_sem.at[i])
        for i, span in enumerate(spans)
    ]
    for copy in known_copies + copies:
        copy.start()
    for copy in known_copies:
        copy.wait()
    slots = table.shape[1]
    lane = lax.broadcasted_iota(jnp.int32, (1, POINTS), 1) % COUNT
    labels = jnp.zeros((1, POINTS), jnp.int32)
    for i in range(COUNT):
        labels = jnp.where(lane == i, table[i // slots, i % slots], labels)
    labels = labels.astype(jnp.float32)
    row = lax.broadcasted_iota(jnp.int32, (COUNT, POINTS), 0)
    weight = jnp.zeros((COUNT, POINTS), jnp.int32)
    for g in range(COUNT // slots):
        weight = jnp.where(row // slots == g, coefs[g], weight)
    weight = weight.astype(jnp.float32)
    for i, copy in enumerate(copies):
        copy.wait()
        for f in range(i * chunk, (i + 1) * chunk):
            out_ref[f * ROWS : f * ROWS + COUNT, :] = grids[:, f, :] * weight
            out_ref[f * ROWS + COUNT : (f + 1) * ROWS, :] = labels


def in_one_row(rows):
    per = POINTS // COUNT
    peer = lax.broadcasted_iota(jnp.int32, (per, POINTS), 0)
    part = lax.broadcasted_iota(jnp.int32, (per, POINTS), 1) // COUNT
    return jnp.concatenate(
        [
            jnp.sum(jnp.where(peer == part, rows[s : s + per], 0.0), axis=0, keepdims=True)
            for s in range(0, PEERS, per)
        ],
        axis=1,
    )


def sum_kernel(got_ref, out_ref):
    labels = in_one_row(
        jnp.concatenate(
            [got_ref[s * ROWS + COUNT : (s + 1) * ROWS, :] for s in range(PEERS)], axis=0
        )
    )
    wanted = lax.broadcasted_iota(jnp.int32, (SUBS, PEERS * COUNT), 0).astype(jnp.float32)
    onehot = (labels == wanted).astype(jnp.float32)
    data = jnp.concatenate(
        [got_ref[s * ROWS : s * ROWS + COUNT, :] for s in range(PEERS)], axis=0
    )
    total = jnp.dot(
        onehot.astype(jnp.bfloat16),
        jnp.concatenate(thirds(data), axis=1),
        preferred_element_type=jnp.float32,
    )
    sparse = total[:, :POINTS] + (
        total[:, POINTS : 2 * POINTS] + total[:, 2 * POINTS :]
    )
    turned = onehot.T.astype(jnp.bfloat16)
    out_ref[...] = jnp.dot(
        jnp.concatenate([turned] * 3, axis=1),
        jnp.concatenate(thirds(sparse), axis=0),
        preferred_element_type=jnp.float32,
    )


def unpack_kernel(back_ref, out_hbm, held, sem):
    chunk = COUNT // CHUNKS
    copies = []
    for i in range(CHUNKS):
        for r in range(i * chunk, (i + 1) * chunk):
            for f in range(0, FIELDS, TILE):
                held[r, f : f + TILE, :] = back_ref[f : f + TILE, r, :]
        span = pl.ds(i * chunk, chunk)
        copies.append(pltpu.make_async_copy(held.at[span], out_hbm.at[span], sem.at[i]))
        copies[-1].start()
    for copy in copies:
        copy.wait()


def on_device(grids, table, coefs):
    f32 = jnp.float32
    messages = pl.pallas_call(
        pack_kernel,
        out_shape=jax.ShapeDtypeStruct((PEERS * ROWS, POINTS), f32),
        in_specs=[HBM, HBM, HBM],
        out_specs=VMEM,
        scratch_shapes=[
            pltpu.SMEM(table.shape, table.dtype),
            pltpu.SMEM(coefs.shape, coefs.dtype),
            pltpu.VMEM((COUNT, FIELDS, POINTS), f32),
            pltpu.SemaphoreType.DMA((2,)),
            pltpu.SemaphoreType.DMA((CHUNKS,)),
        ],
        compiler_params=ROOM,
    )(*map(in_hbm, (table, coefs, grids.reshape(COUNT, FIELDS, POINTS))))
    got = lax.all_to_all(messages.reshape(PEERS, 1, ROWS * POINTS), "grp", 0, 0, tiled=True)
    picks = pl.pallas_call(
        sum_kernel,
        out_shape=jax.ShapeDtypeStruct((PEERS * COUNT, POINTS), f32),
        in_specs=[VMEM],
        out_specs=VMEM,
        compiler_params=ROOM,
    )(got.reshape(PEERS * ROWS, POINTS))
    back = lax.all_to_all(picks.reshape(PEERS, COUNT, POINTS), "grp", 0, 0, tiled=True)
    combined = pl.pallas_call(
        unpack_kernel,
        out_shape=jax.ShapeDtypeStruct((COUNT, FIELDS, POINTS), f32),
        in_specs=[VMEM],
        out_specs=HBM,
        scratch_shapes=[
            pltpu.VMEM((COUNT, FIELDS, POINTS), f32),
            pltpu.SemaphoreType.DMA((CHUNKS,)),
        ],
        compiler_params=ROOM,
    )(back)
    return combined.reshape(grids.shape)


def solution(mesh):
    return jax.shard_map(
        on_device,
        mesh=mesh,
        in_specs=(P("grp", None, None, "dom"), P("grp", None), P("grp")),
        out_specs=P("grp", None, None, "dom"),
        check_vma=False,
    )
```

```python
import jax
import jax.numpy as jnp
from jax import lax
from jax.experimental import pallas as pl
from jax.experimental.pallas import tpu as pltpu
from jax.sharding import PartitionSpec as P

SUBS = 64
Y, Z, CORES = 8, 4, 2
PLANES = [[(y * Z + z) * CORES + c for y in range(Y) for c in range(CORES)] for z in range(Z)]
COLUMNS = [[(y * Z + z) * CORES + c for z in range(Z)] for y in range(Y) for c in range(CORES)]
PEERS = Y * CORES
COUNT = 16
FIELDS = 64
POINTS = 128
OWN = FIELDS // PEERS
ROWS = OWN * COUNT
MESSAGE = ROWS + 1
TILE = 8
CHUNKS = 4
VMEM = pl.BlockSpec(memory_space=pltpu.VMEM)
ROOM = pltpu.CompilerParams(vmem_limit_bytes=8 << 20)
HBM = pl.BlockSpec(memory_space=pltpu.HBM)


def exchange(value):
    return lax.all_to_all(value, "grp", 0, 0, tiled=True, axis_index_groups=PLANES)


def in_hbm(value):
    return pltpu.with_memory_space_constraint(value, pltpu.HBM)


def thirds(value):
    high = value.astype(jnp.bfloat16)
    rest = value - high.astype(jnp.float32)
    mid = rest.astype(jnp.bfloat16)
    low = (rest - mid.astype(jnp.float32)).astype(jnp.bfloat16)
    return high, mid, low


def pack_kernel(table_hbm, coefs_hbm, grids_hbm, out_ref, table, coefs, grids, known_sem, grids_sem):
    known_copies = [
        pltpu.make_async_copy(table_hbm, table, known_sem.at[0]),
        pltpu.make_async_copy(coefs_hbm, coefs, known_sem.at[1]),
    ]
    chunk = FIELDS // CHUNKS
    spans = [pl.ds(i * chunk, chunk) for i in range(CHUNKS)]
    copies = [
        pltpu.make_async_copy(grids_hbm.at[:, span, :], grids.at[:, span, :], grids_sem.at[i])
        for i, span in enumerate(spans)
    ]
    for copy in known_copies + copies:
        copy.start()
    for copy in known_copies:
        copy.wait()
    slots = table.shape[1]
    lane = lax.broadcasted_iota(jnp.int32, (1, POINTS), 1) % COUNT
    labels = jnp.zeros((1, POINTS), jnp.int32)
    for i in range(COUNT):
        labels = jnp.where(lane == i, table[i // slots, i % slots], labels)
    labels = labels.astype(jnp.float32)
    row = lax.broadcasted_iota(jnp.int32, (COUNT, POINTS), 0)
    weight = jnp.zeros((COUNT, POINTS), jnp.int32)
    for g in range(COUNT // slots):
        weight = jnp.where(row // slots == g, coefs[g], weight)
    weight = weight.astype(jnp.float32)
    for peer in range(PEERS):
        out_ref[peer * MESSAGE + ROWS : (peer + 1) * MESSAGE, :] = labels
    for i, copy in enumerate(copies):
        copy.wait()
        for f in range(i * chunk, (i + 1) * chunk):
            peer, j = divmod(f, OWN)
            at = peer * MESSAGE + j * COUNT
            out_ref[at : at + COUNT, :] = grids[:, f, :] * weight


def in_one_row(rows):
    peer = lax.broadcasted_iota(jnp.int32, rows.shape, 0)
    part = lax.broadcasted_iota(jnp.int32, rows.shape, 1) // COUNT
    per = POINTS // COUNT
    return jnp.concatenate(
        [
            jnp.sum(jnp.where(peer == part + h * per, rows, 0.0), axis=0, keepdims=True)
            for h in range(PEERS // per)
        ],
        axis=1,
    )


def sum_kernel(got_ref, out_ref, labels_ref):
    labels = in_one_row(
        jnp.concatenate(
            [got_ref[(s + 1) * MESSAGE - 1 : (s + 1) * MESSAGE, :] for s in range(PEERS)], axis=0
        )
    )
    wanted = lax.broadcasted_iota(jnp.int32, (SUBS, PEERS * COUNT), 0).astype(jnp.float32)
    onehot = (labels == wanted).astype(jnp.float32).astype(jnp.bfloat16)

    def rows_of(s, j):
        at = s * MESSAGE + j * COUNT
        return got_ref[at : at + COUNT, :]

    data = jnp.concatenate(
        [
            jnp.concatenate([rows_of(s, j) for s in range(PEERS)], axis=0)
            for j in range(OWN)
        ],
        axis=1,
    )
    high, mid, low = (
        jnp.dot(onehot, part, preferred_element_type=jnp.float32) for part in thirds(data)
    )
    total = high + (mid + low)
    for j in range(OWN):
        out_ref[j] = total[:, j * POINTS : (j + 1) * POINTS]
    labels_ref[...] = jnp.broadcast_to(labels, labels_ref.shape)


def pick_kernel(every_ref, labels_ref, out_ref):
    sparse = jnp.concatenate(
        [
            (every_ref[0, j] + every_ref[1, j]) + (every_ref[2, j] + every_ref[3, j])
            for j in range(OWN)
        ],
        axis=1,
    )
    wanted = lax.broadcasted_iota(jnp.int32, (SUBS, PEERS * COUNT), 0).astype(jnp.float32)
    onehot = (labels_ref[0:1, :] == wanted).astype(jnp.float32).T.astype(jnp.bfloat16)
    picks = jnp.dot(
        jnp.concatenate([onehot] * 3, axis=1),
        jnp.concatenate(thirds(sparse), axis=0),
        preferred_element_type=jnp.float32,
    )
    for j in range(OWN):
        out_ref[:, j * COUNT : (j + 1) * COUNT, :] = picks[
            :, j * POINTS : (j + 1) * POINTS
        ].reshape(PEERS, COUNT, POINTS)


def unpack_kernel(back_ref, out_hbm, held, sem):
    chunk = COUNT // CHUNKS
    copies = []
    for i in range(CHUNKS):
        for r in range(i * chunk, (i + 1) * chunk):
            for f in range(0, FIELDS, TILE):
                held[r, f : f + TILE, :] = back_ref[f : f + TILE, r, :]
        span = pl.ds(i * chunk, chunk)
        copies.append(pltpu.make_async_copy(held.at[span], out_hbm.at[span], sem.at[i]))
        copies[-1].start()
    for copy in copies:
        copy.wait()


def on_device(grids, table, coefs):
    f32 = jnp.float32
    messages = pl.pallas_call(
        pack_kernel,
        out_shape=jax.ShapeDtypeStruct((PEERS * MESSAGE, POINTS), f32),
        in_specs=[HBM, HBM, HBM],
        out_specs=VMEM,
        scratch_shapes=[
            pltpu.SMEM(table.shape, table.dtype),
            pltpu.SMEM(coefs.shape, coefs.dtype),
            pltpu.VMEM((COUNT, FIELDS, POINTS), f32),
            pltpu.SemaphoreType.DMA((2,)),
            pltpu.SemaphoreType.DMA((CHUNKS,)),
        ],
        compiler_params=ROOM,
    )(*map(in_hbm, (table, coefs, grids.reshape(COUNT, FIELDS, POINTS))))
    got = exchange(messages.reshape(PEERS, 1, MESSAGE * POINTS))
    partial, labels = pl.pallas_call(
        sum_kernel,
        out_shape=(
            jax.ShapeDtypeStruct((OWN, SUBS, POINTS), f32),
            jax.ShapeDtypeStruct((TILE, PEERS * COUNT), f32),
        ),
        in_specs=[VMEM],
        out_specs=(VMEM, VMEM),
        compiler_params=ROOM,
    )(got.reshape(PEERS * MESSAGE, POINTS))
    every = lax.all_gather(partial, "grp", axis_index_groups=COLUMNS)
    picks = pl.pallas_call(
        pick_kernel,
        out_shape=jax.ShapeDtypeStruct((PEERS, ROWS, POINTS), f32),
        in_specs=[VMEM, VMEM],
        out_specs=VMEM,
        compiler_params=ROOM,
    )(every, labels)
    back = exchange(picks).reshape(FIELDS, COUNT, POINTS)
    combined = pl.pallas_call(
        unpack_kernel,
        out_shape=jax.ShapeDtypeStruct((COUNT, FIELDS, POINTS), f32),
        in_specs=[VMEM],
        out_specs=HBM,
        scratch_shapes=[
            pltpu.VMEM((COUNT, FIELDS, POINTS), f32),
            pltpu.SemaphoreType.DMA((CHUNKS,)),
        ],
        compiler_params=ROOM,
    )(back)
    return combined.reshape(grids.shape)


def solution(mesh):
    return jax.shard_map(
        on_device,
        mesh=mesh,
        in_specs=(P("grp", None, None, "dom"), P("grp", None), P("grp")),
        out_specs=P("grp", None, None, "dom"),
        check_vma=False,
    )
```

```python
import jax
import jax.numpy as jnp
from jax import lax
from jax.experimental import pallas as pl
from jax.experimental.pallas import tpu as pltpu
from jax.sharding import PartitionSpec as P

SUBS = 64
Y, Z, CORES = 8, 4, 2
PLANES = [[(y * Z + z) * CORES + c for y in range(Y) for c in range(CORES)] for z in range(Z)]
LINES = [[(y * Z + z) * CORES + c for y in range(Y)] for z in range(Z) for c in range(CORES)]
SIBLINGS = [(i, i ^ 1) for i in range(Y * Z * CORES)]
COLUMNS = [[(y * Z + z) * CORES + c for z in range(Z)] for y in range(Y) for c in range(CORES)]
PEERS = Y * CORES
COUNT = 16
FIELDS = 64
POINTS = 128
OWN = FIELDS // PEERS
ROWS = OWN * COUNT
BOTH = CORES * OWN
MESSAGE = BOTH * COUNT + 1
TILE = 8
CHUNKS = 4
VMEM = pl.BlockSpec(memory_space=pltpu.VMEM)
ROOM = pltpu.CompilerParams(vmem_limit_bytes=8 << 20)
HBM = pl.BlockSpec(memory_space=pltpu.HBM)


def exchange(value, groups):
    return lax.all_to_all(value, "grp", 0, 0, tiled=True, axis_index_groups=groups)


def in_hbm(value):
    return pltpu.with_memory_space_constraint(value, pltpu.HBM)


def thirds(value):
    high = value.astype(jnp.bfloat16)
    rest = value - high.astype(jnp.float32)
    mid = rest.astype(jnp.bfloat16)
    low = (rest - mid.astype(jnp.float32)).astype(jnp.bfloat16)
    return high, mid, low


def pack_kernel(table_hbm, coefs_hbm, grids_hbm, out_ref, table, coefs, grids, known_sem, grids_sem):
    known_copies = [
        pltpu.make_async_copy(table_hbm, table, known_sem.at[0]),
        pltpu.make_async_copy(coefs_hbm, coefs, known_sem.at[1]),
    ]
    chunk = FIELDS // CHUNKS
    spans = [pl.ds(i * chunk, chunk) for i in range(CHUNKS)]
    copies = [
        pltpu.make_async_copy(grids_hbm.at[:, span, :], grids.at[:, span, :], grids_sem.at[i])
        for i, span in enumerate(spans)
    ]
    for copy in known_copies + copies:
        copy.start()
    for copy in known_copies:
        copy.wait()
    slots = table.shape[1]
    lane = lax.broadcasted_iota(jnp.int32, (1, POINTS), 1) % COUNT
    labels = jnp.zeros((1, POINTS), jnp.int32)
    for i in range(COUNT):
        labels = jnp.where(lane == i, table[i // slots, i % slots], labels)
    labels = labels.astype(jnp.float32)
    row = lax.broadcasted_iota(jnp.int32, (COUNT, POINTS), 0)
    weight = jnp.zeros((COUNT, POINTS), jnp.int32)
    for g in range(COUNT // slots):
        weight = jnp.where(row // slots == g, coefs[g], weight)
    weight = weight.astype(jnp.float32)
    for peer in range(Y):
        out_ref[(peer + 1) * MESSAGE - 1 : (peer + 1) * MESSAGE, :] = labels
    for i, copy in enumerate(copies):
        copy.wait()
        for f in range(i * chunk, (i + 1) * chunk):
            peer, j = divmod(f, BOTH)
            at = peer * MESSAGE + j * COUNT
            out_ref[at : at + COUNT, :] = grids[:, f, :] * weight


def sum_kernel(got_ref, mine_ref, theirs_ref, labels_ref):
    first_core = lax.axis_index("grp") % CORES == 0
    rows = jnp.concatenate(
        [got_ref[(s + 1) * MESSAGE - 1 : (s + 1) * MESSAGE, :] for s in range(Y)], axis=0
    )
    peer = lax.broadcasted_iota(jnp.int32, rows.shape, 0)
    part = lax.broadcasted_iota(jnp.int32, rows.shape, 1) // COUNT
    labels = jnp.sum(jnp.where(peer == part, rows, 0.0), axis=0, keepdims=True)
    wanted = lax.broadcasted_iota(jnp.int32, (SUBS, Y * COUNT), 0).astype(jnp.float32)
    onehot = (labels == wanted).astype(jnp.float32).astype(jnp.bfloat16)

    def rows_of(s, j):
        at = s * MESSAGE + j * COUNT
        return got_ref[at : at + COUNT, :]

    data = jnp.concatenate(
        [jnp.concatenate([rows_of(s, j) for s in range(Y)], axis=0) for j in range(BOTH)],
        axis=1,
    )
    high, mid, low = (
        jnp.dot(onehot, part, preferred_element_type=jnp.float32) for part in thirds(data)
    )
    total = high + (mid + low)
    for j in range(OWN):
        first = total[:, j * POINTS : (j + 1) * POINTS]
        second = total[:, (OWN + j) * POINTS : (OWN + j + 1) * POINTS]
        mine_ref[j * SUBS : (j + 1) * SUBS, :] = jnp.where(first_core, first, second)
        theirs_ref[j * SUBS : (j + 1) * SUBS, :] = jnp.where(first_core, second, first)
    labels_ref[...] = jnp.broadcast_to(labels, labels_ref.shape)
    theirs_ref[OWN * SUBS :, :] = jnp.broadcast_to(labels, (TILE, POINTS))


def pick_kernel(every_ref, labels_ref, from_sibling_ref, out_ref):
    first_core = lax.axis_index("grp") % CORES == 0
    sparse = jnp.concatenate(
        [
            (every_ref[0, part] + every_ref[1, part]) + (every_ref[2, part] + every_ref[3, part])
            for part in (slice(j * SUBS, (j + 1) * SUBS) for j in range(OWN))
        ],
        axis=1,
    )
    own = labels_ref[0:1, :]
    sibling = from_sibling_ref[OWN * SUBS : OWN * SUBS + 1, :]
    labels = jnp.concatenate(
        [jnp.where(first_core, own, sibling), jnp.where(first_core, sibling, own)], axis=1
    )
    wanted = lax.broadcasted_iota(jnp.int32, (SUBS, PEERS * COUNT), 0).astype(jnp.float32)
    onehot = (labels == wanted).astype(jnp.float32).T.astype(jnp.bfloat16)
    picks = jnp.dot(
        jnp.concatenate([onehot] * 3, axis=1),
        jnp.concatenate(thirds(sparse), axis=0),
        preferred_element_type=jnp.float32,
    )
    for c in range(CORES):
        for y in range(Y):
            at = (c * Y + y) * COUNT
            for j in range(OWN):
                out_ref[y * CORES + c, j * COUNT : (j + 1) * COUNT, :] = picks[
                    at : at + COUNT, j * POINTS : (j + 1) * POINTS
                ]


def unpack_kernel(back_ref, out_hbm, held, sem):
    chunk = COUNT // CHUNKS
    copies = []
    for i in range(CHUNKS):
        for r in range(i * chunk, (i + 1) * chunk):
            for f in range(0, FIELDS, TILE):
                held[r, f : f + TILE, :] = back_ref[f : f + TILE, r, :]
        span = pl.ds(i * chunk, chunk)
        copies.append(pltpu.make_async_copy(held.at[span], out_hbm.at[span], sem.at[i]))
        copies[-1].start()
    for copy in copies:
        copy.wait()


def on_device(grids, table, coefs):
    f32 = jnp.float32
    messages = pl.pallas_call(
        pack_kernel,
        out_shape=jax.ShapeDtypeStruct((Y * MESSAGE, POINTS), f32),
        in_specs=[HBM, HBM, HBM],
        out_specs=VMEM,
        scratch_shapes=[
            pltpu.SMEM(table.shape, table.dtype),
            pltpu.SMEM(coefs.shape, coefs.dtype),
            pltpu.VMEM((COUNT, FIELDS, POINTS), f32),
            pltpu.SemaphoreType.DMA((2,)),
            pltpu.SemaphoreType.DMA((CHUNKS,)),
        ],
        compiler_params=ROOM,
    )(*map(in_hbm, (table, coefs, grids.reshape(COUNT, FIELDS, POINTS))))
    got = exchange(messages.reshape(Y, 1, MESSAGE * POINTS), LINES)
    mine, theirs, labels = pl.pallas_call(
        sum_kernel,
        out_shape=(
            jax.ShapeDtypeStruct((OWN * SUBS, POINTS), f32),
            jax.ShapeDtypeStruct((OWN * SUBS + TILE, POINTS), f32),
            jax.ShapeDtypeStruct((TILE, POINTS), f32),
        ),
        in_specs=[VMEM],
        out_specs=(VMEM, VMEM, VMEM),
        compiler_params=ROOM,
    )(got.reshape(Y * MESSAGE, POINTS))
    from_sibling = lax.ppermute(theirs, "grp", SIBLINGS)
    partial = mine + from_sibling[: OWN * SUBS]
    every = lax.all_gather(partial, "grp", axis_index_groups=COLUMNS)
    picks = pl.pallas_call(
        pick_kernel,
        out_shape=jax.ShapeDtypeStruct((PEERS, ROWS, POINTS), f32),
        in_specs=[VMEM, VMEM, VMEM],
        out_specs=VMEM,
        compiler_params=ROOM,
    )(every, labels, from_sibling)
    back = exchange(picks, PLANES).reshape(FIELDS, COUNT, POINTS)
    combined = pl.pallas_call(
        unpack_kernel,
        out_shape=jax.ShapeDtypeStruct((COUNT, FIELDS, POINTS), f32),
        in_specs=[VMEM],
        out_specs=HBM,
        scratch_shapes=[
            pltpu.VMEM((COUNT, FIELDS, POINTS), f32),
            pltpu.SemaphoreType.DMA((CHUNKS,)),
        ],
        compiler_params=ROOM,
    )(back)
    return combined.reshape(grids.shape)


def solution(mesh):
    return jax.shard_map(
        on_device,
        mesh=mesh,
        in_specs=(P("grp", None, None, "dom"), P("grp", None), P("grp")),
        out_specs=P("grp", None, None, "dom"),
        check_vma=False,
    )
```

```python
import jax
import jax.numpy as jnp
from jax import lax
from jax.experimental import pallas as pl
from jax.experimental.pallas import tpu as pltpu
from jax.sharding import PartitionSpec as P

SUBS = 64
Y, Z, CORES = 8, 4, 2
PLANES = [[(y * Z + z) * CORES + c for y in range(Y) for c in range(CORES)] for z in range(Z)]


def partners(turn):
    pairs = []
    for i in range(Y * Z * CORES):
        y, z, c = i // (Z * CORES), i // CORES % Z, i % CORES
        other = z ^ 1 if turn == c else Z - 1 - z
        pairs.append((i, (y * Z + other) * CORES + c))
    return pairs


PEERS = Y * CORES
COUNT = 16
FIELDS = 64
POINTS = 128
OWN = FIELDS // PEERS
ROWS = OWN * COUNT
MESSAGE = ROWS + 1
TILE = 8
CHUNKS = 4
VMEM = pl.BlockSpec(memory_space=pltpu.VMEM)
ROOM = pltpu.CompilerParams(vmem_limit_bytes=8 << 20)
HBM = pl.BlockSpec(memory_space=pltpu.HBM)


def exchange(value):
    return lax.all_to_all(value, "grp", 0, 0, tiled=True, axis_index_groups=PLANES)


def in_hbm(value):
    return pltpu.with_memory_space_constraint(value, pltpu.HBM)


def thirds(value):
    high = value.astype(jnp.bfloat16)
    rest = value - high.astype(jnp.float32)
    mid = rest.astype(jnp.bfloat16)
    low = (rest - mid.astype(jnp.float32)).astype(jnp.bfloat16)
    return high, mid, low


def pack_kernel(table_hbm, coefs_hbm, grids_hbm, out_ref, table, coefs, grids, known_sem, grids_sem):
    known_copies = [
        pltpu.make_async_copy(table_hbm, table, known_sem.at[0]),
        pltpu.make_async_copy(coefs_hbm, coefs, known_sem.at[1]),
    ]
    chunk = FIELDS // CHUNKS
    spans = [pl.ds(i * chunk, chunk) for i in range(CHUNKS)]
    copies = [
        pltpu.make_async_copy(grids_hbm.at[:, span, :], grids.at[:, span, :], grids_sem.at[i])
        for i, span in enumerate(spans)
    ]
    for copy in known_copies + copies:
        copy.start()
    for copy in known_copies:
        copy.wait()
    slots = table.shape[1]
    lane = lax.broadcasted_iota(jnp.int32, (1, POINTS), 1) % COUNT
    labels = jnp.zeros((1, POINTS), jnp.int32)
    for i in range(COUNT):
        labels = jnp.where(lane == i, table[i // slots, i % slots], labels)
    labels = labels.astype(jnp.float32)
    row = lax.broadcasted_iota(jnp.int32, (COUNT, POINTS), 0)
    weight = jnp.zeros((COUNT, POINTS), jnp.int32)
    for g in range(COUNT // slots):
        weight = jnp.where(row // slots == g, coefs[g], weight)
    weight = weight.astype(jnp.float32)
    for peer in range(PEERS):
        out_ref[peer * MESSAGE + ROWS : (peer + 1) * MESSAGE, :] = labels
    for i, copy in enumerate(copies):
        copy.wait()
        for f in range(i * chunk, (i + 1) * chunk):
            peer, j = divmod(f, OWN)
            at = peer * MESSAGE + j * COUNT
            out_ref[at : at + COUNT, :] = grids[:, f, :] * weight


def in_one_row(rows):
    peer = lax.broadcasted_iota(jnp.int32, rows.shape, 0)
    part = lax.broadcasted_iota(jnp.int32, rows.shape, 1) // COUNT
    per = POINTS // COUNT
    return jnp.concatenate(
        [
            jnp.sum(jnp.where(peer == part + h * per, rows, 0.0), axis=0, keepdims=True)
            for h in range(PEERS // per)
        ],
        axis=1,
    )


def sum_kernel(got_ref, out_ref, labels_ref):
    labels = in_one_row(
        jnp.concatenate(
            [got_ref[(s + 1) * MESSAGE - 1 : (s + 1) * MESSAGE, :] for s in range(PEERS)], axis=0
        )
    )
    wanted = lax.broadcasted_iota(jnp.int32, (SUBS, PEERS * COUNT), 0).astype(jnp.float32)
    onehot = (labels == wanted).astype(jnp.float32).astype(jnp.bfloat16)

    def rows_of(s, j):
        at = s * MESSAGE + j * COUNT
        return got_ref[at : at + COUNT, :]

    data = jnp.concatenate(
        [
            jnp.concatenate([rows_of(s, j) for s in range(PEERS)], axis=0)
            for j in range(OWN)
        ],
        axis=1,
    )
    high, mid, low = (
        jnp.dot(onehot, part, preferred_element_type=jnp.float32) for part in thirds(data)
    )
    total = high + (mid + low)
    for j in range(OWN):
        out_ref[j] = total[:, j * POINTS : (j + 1) * POINTS]
    labels_ref[...] = jnp.broadcast_to(labels, labels_ref.shape)


def pick_kernel(pair_ref, other_pair_ref, labels_ref, out_ref):
    sparse = jnp.concatenate([pair_ref[j] + other_pair_ref[j] for j in range(OWN)], axis=1)
    wanted = lax.broadcasted_iota(jnp.int32, (SUBS, PEERS * COUNT), 0).astype(jnp.float32)
    onehot = (labels_ref[0:1, :] == wanted).astype(jnp.float32).T.astype(jnp.bfloat16)
    picks = jnp.dot(
        jnp.concatenate([onehot] * 3, axis=1),
        jnp.concatenate(thirds(sparse), axis=0),
        preferred_element_type=jnp.float32,
    )
    for j in range(OWN):
        out_ref[:, j * COUNT : (j + 1) * COUNT, :] = picks[
            :, j * POINTS : (j + 1) * POINTS
        ].reshape(PEERS, COUNT, POINTS)


def unpack_kernel(back_ref, out_hbm, held, sem):
    chunk = COUNT // CHUNKS
    copies = []
    for i in range(CHUNKS):
        for r in range(i * chunk, (i + 1) * chunk):
            for f in range(0, FIELDS, TILE):
                held[r, f : f + TILE, :] = back_ref[f : f + TILE, r, :]
        span = pl.ds(i * chunk, chunk)
        copies.append(pltpu.make_async_copy(held.at[span], out_hbm.at[span], sem.at[i]))
        copies[-1].start()
    for copy in copies:
        copy.wait()


def on_device(grids, table, coefs):
    f32 = jnp.float32
    messages = pl.pallas_call(
        pack_kernel,
        out_shape=jax.ShapeDtypeStruct((PEERS * MESSAGE, POINTS), f32),
        in_specs=[HBM, HBM, HBM],
        out_specs=VMEM,
        scratch_shapes=[
            pltpu.SMEM(table.shape, table.dtype),
            pltpu.SMEM(coefs.shape, coefs.dtype),
            pltpu.VMEM((COUNT, FIELDS, POINTS), f32),
            pltpu.SemaphoreType.DMA((2,)),
            pltpu.SemaphoreType.DMA((CHUNKS,)),
        ],
        compiler_params=ROOM,
    )(*map(in_hbm, (table, coefs, grids.reshape(COUNT, FIELDS, POINTS))))
    got = exchange(messages.reshape(PEERS, 1, MESSAGE * POINTS))
    partial, labels = pl.pallas_call(
        sum_kernel,
        out_shape=(
            jax.ShapeDtypeStruct((OWN, SUBS, POINTS), f32),
            jax.ShapeDtypeStruct((TILE, PEERS * COUNT), f32),
        ),
        in_specs=[VMEM],
        out_specs=(VMEM, VMEM),
        compiler_params=ROOM,
    )(got.reshape(PEERS * MESSAGE, POINTS))
    pair = partial + lax.ppermute(partial, "grp", partners(0))
    other_pair = lax.ppermute(pair, "grp", partners(1))
    picks = pl.pallas_call(
        pick_kernel,
        out_shape=jax.ShapeDtypeStruct((PEERS, ROWS, POINTS), f32),
        in_specs=[VMEM, VMEM, VMEM],
        out_specs=VMEM,
        compiler_params=ROOM,
    )(pair, other_pair, labels)
    back = exchange(picks).reshape(FIELDS, COUNT, POINTS)
    combined = pl.pallas_call(
        unpack_kernel,
        out_shape=jax.ShapeDtypeStruct((COUNT, FIELDS, POINTS), f32),
        in_specs=[VMEM],
        out_specs=HBM,
        scratch_shapes=[
            pltpu.VMEM((COUNT, FIELDS, POINTS), f32),
            pltpu.SemaphoreType.DMA((CHUNKS,)),
        ],
        compiler_params=ROOM,
    )(back)
    return combined.reshape(grids.shape)


def solution(mesh):
    return jax.shard_map(
        on_device,
        mesh=mesh,
        in_specs=(P("grp", None, None, "dom"), P("grp", None), P("grp")),
        out_specs=P("grp", None, None, "dom"),
        check_vma=False,
    )
```

```python
import jax
import jax.numpy as jnp
from jax import lax
from jax.experimental import pallas as pl
from jax.experimental.pallas import tpu as pltpu
from jax.sharding import PartitionSpec as P

SUBS = 64
Y, Z, CORES = 8, 4, 2
PLANES = [[(y * Z + z) * CORES + c for y in range(Y) for c in range(CORES)] for z in range(Z)]


def along_z(step):
    places = [(y, z, c) for y in range(Y) for z in range(Z) for c in range(CORES)]
    return [(i, (y * Z + (z + step) % Z) * CORES + c) for i, (y, z, c) in enumerate(places)]


PEERS = Y * CORES
COUNT = 16
FIELDS = 64
POINTS = 128
OWN = FIELDS // PEERS
ROWS = OWN * COUNT
MESSAGE = ROWS + 1
TILE = 8
CHUNKS = 4
VMEM = pl.BlockSpec(memory_space=pltpu.VMEM)
ROOM = pltpu.CompilerParams(vmem_limit_bytes=8 << 20)
HBM = pl.BlockSpec(memory_space=pltpu.HBM)


def exchange(value):
    return lax.all_to_all(value, "grp", 0, 0, tiled=True, axis_index_groups=PLANES)


def in_hbm(value):
    return pltpu.with_memory_space_constraint(value, pltpu.HBM)


def thirds(value):
    high = value.astype(jnp.bfloat16)
    rest = value - high.astype(jnp.float32)
    mid = rest.astype(jnp.bfloat16)
    low = (rest - mid.astype(jnp.float32)).astype(jnp.bfloat16)
    return high, mid, low


def pack_kernel(table_hbm, coefs_hbm, grids_hbm, out_ref, table, coefs, grids, known_sem, grids_sem):
    known_copies = [
        pltpu.make_async_copy(table_hbm, table, known_sem.at[0]),
        pltpu.make_async_copy(coefs_hbm, coefs, known_sem.at[1]),
    ]
    chunk = FIELDS // CHUNKS
    spans = [pl.ds(i * chunk, chunk) for i in range(CHUNKS)]
    copies = [
        pltpu.make_async_copy(grids_hbm.at[:, span, :], grids.at[:, span, :], grids_sem.at[i])
        for i, span in enumerate(spans)
    ]
    for copy in known_copies + copies:
        copy.start()
    for copy in known_copies:
        copy.wait()
    slots = table.shape[1]
    lane = lax.broadcasted_iota(jnp.int32, (1, POINTS), 1) % COUNT
    labels = jnp.zeros((1, POINTS), jnp.int32)
    for i in range(COUNT):
        labels = jnp.where(lane == i, table[i // slots, i % slots], labels)
    labels = labels.astype(jnp.float32)
    row = lax.broadcasted_iota(jnp.int32, (COUNT, POINTS), 0)
    weight = jnp.zeros((COUNT, POINTS), jnp.int32)
    for g in range(COUNT // slots):
        weight = jnp.where(row // slots == g, coefs[g], weight)
    weight = weight.astype(jnp.float32)
    for peer in range(PEERS):
        out_ref[peer * MESSAGE + ROWS : (peer + 1) * MESSAGE, :] = labels
    for i, copy in enumerate(copies):
        copy.wait()
        for f in range(i * chunk, (i + 1) * chunk):
            peer, j = divmod(f, OWN)
            at = peer * MESSAGE + j * COUNT
            out_ref[at : at + COUNT, :] = grids[:, f, :] * weight


def in_one_row(rows):
    peer = lax.broadcasted_iota(jnp.int32, rows.shape, 0)
    part = lax.broadcasted_iota(jnp.int32, rows.shape, 1) // COUNT
    per = POINTS // COUNT
    return jnp.concatenate(
        [
            jnp.sum(jnp.where(peer == part + h * per, rows, 0.0), axis=0, keepdims=True)
            for h in range(PEERS // per)
        ],
        axis=1,
    )


def sum_kernel(got_ref, out_ref, labels_ref):
    labels = in_one_row(
        jnp.concatenate(
            [got_ref[(s + 1) * MESSAGE - 1 : (s + 1) * MESSAGE, :] for s in range(PEERS)], axis=0
        )
    )
    wanted = lax.broadcasted_iota(jnp.int32, (SUBS, PEERS * COUNT), 0).astype(jnp.float32)
    onehot = (labels == wanted).astype(jnp.float32).astype(jnp.bfloat16)

    def rows_of(s, j):
        at = s * MESSAGE + j * COUNT
        return got_ref[at : at + COUNT, :]

    data = jnp.concatenate(
        [
            jnp.concatenate([rows_of(s, j) for s in range(PEERS)], axis=0)
            for j in range(OWN)
        ],
        axis=1,
    )
    high, mid, low = (
        jnp.dot(onehot, part, preferred_element_type=jnp.float32) for part in thirds(data)
    )
    total = high + (mid + low)
    for j in range(OWN):
        out_ref[j] = total[:, j * POINTS : (j + 1) * POINTS]
    labels_ref[...] = jnp.broadcast_to(labels, labels_ref.shape)


def pick_kernel(own_ref, far_ref, below_ref, above_ref, labels_ref, out_ref):
    sparse = jnp.concatenate(
        [(own_ref[j] + far_ref[j]) + (below_ref[j] + above_ref[j]) for j in range(OWN)], axis=1
    )
    wanted = lax.broadcasted_iota(jnp.int32, (SUBS, PEERS * COUNT), 0).astype(jnp.float32)
    onehot = (labels_ref[0:1, :] == wanted).astype(jnp.float32).T.astype(jnp.bfloat16)
    picks = jnp.dot(
        jnp.concatenate([onehot] * 3, axis=1),
        jnp.concatenate(thirds(sparse), axis=0),
        preferred_element_type=jnp.float32,
    )
    for j in range(OWN):
        out_ref[:, j * COUNT : (j + 1) * COUNT, :] = picks[
            :, j * POINTS : (j + 1) * POINTS
        ].reshape(PEERS, COUNT, POINTS)


def unpack_kernel(back_ref, out_hbm, held, sem):
    chunk = COUNT // CHUNKS
    copies = []
    for i in range(CHUNKS):
        for r in range(i * chunk, (i + 1) * chunk):
            for f in range(0, FIELDS, TILE):
                held[r, f : f + TILE, :] = back_ref[f : f + TILE, r, :]
        span = pl.ds(i * chunk, chunk)
        copies.append(pltpu.make_async_copy(held.at[span], out_hbm.at[span], sem.at[i]))
        copies[-1].start()
    for copy in copies:
        copy.wait()


def on_device(grids, table, coefs):
    f32 = jnp.float32
    messages = pl.pallas_call(
        pack_kernel,
        out_shape=jax.ShapeDtypeStruct((PEERS * MESSAGE, POINTS), f32),
        in_specs=[HBM, HBM, HBM],
        out_specs=VMEM,
        scratch_shapes=[
            pltpu.SMEM(table.shape, table.dtype),
            pltpu.SMEM(coefs.shape, coefs.dtype),
            pltpu.VMEM((COUNT, FIELDS, POINTS), f32),
            pltpu.SemaphoreType.DMA((2,)),
            pltpu.SemaphoreType.DMA((CHUNKS,)),
        ],
        compiler_params=ROOM,
    )(*map(in_hbm, (table, coefs, grids.reshape(COUNT, FIELDS, POINTS))))
    got = exchange(messages.reshape(PEERS, 1, MESSAGE * POINTS))
    partial, labels = pl.pallas_call(
        sum_kernel,
        out_shape=(
            jax.ShapeDtypeStruct((OWN, SUBS, POINTS), f32),
            jax.ShapeDtypeStruct((TILE, PEERS * COUNT), f32),
        ),
        in_specs=[VMEM],
        out_specs=(VMEM, VMEM),
        compiler_params=ROOM,
    )(got.reshape(PEERS * MESSAGE, POINTS))
    others = [lax.ppermute(partial, "grp", along_z(step)) for step in (2, 1, 3)]
    picks = pl.pallas_call(
        pick_kernel,
        out_shape=jax.ShapeDtypeStruct((PEERS, ROWS, POINTS), f32),
        in_specs=[VMEM] * 5,
        out_specs=VMEM,
        compiler_params=ROOM,
    )(partial, *others, labels)
    back = exchange(picks).reshape(FIELDS, COUNT, POINTS)
    combined = pl.pallas_call(
        unpack_kernel,
        out_shape=jax.ShapeDtypeStruct((COUNT, FIELDS, POINTS), f32),
        in_specs=[VMEM],
        out_specs=HBM,
        scratch_shapes=[
            pltpu.VMEM((COUNT, FIELDS, POINTS), f32),
            pltpu.SemaphoreType.DMA((CHUNKS,)),
        ],
        compiler_params=ROOM,
    )(back)
    return combined.reshape(grids.shape)


def solution(mesh):
    return jax.shard_map(
        on_device,
        mesh=mesh,
        in_specs=(P("grp", None, None, "dom"), P("grp", None), P("grp")),
        out_specs=P("grp", None, None, "dom"),
        check_vma=False,
    )
```

```python
import jax
import jax.numpy as jnp
from jax import lax
from jax.experimental import pallas as pl
from jax.experimental.pallas import tpu as pltpu
from jax.sharding import PartitionSpec as P

SUBS = 64
Y, Z, CORES = 8, 4, 2
PLANES = [[(y * Z + z) * CORES + c for y in range(Y) for c in range(CORES)] for z in range(Z)]


def partners(turn):
    pairs = []
    for i in range(Y * Z * CORES):
        y, z, c = i // (Z * CORES), i // CORES % Z, i % CORES
        other = ((z ^ 2, Z - 1 - z), (Z - 1 - z, z ^ 1))[c][turn]
        pairs.append((i, (y * Z + other) * CORES + c))
    return pairs


PEERS = Y * CORES
COUNT = 16
FIELDS = 64
POINTS = 128
OWN = FIELDS // PEERS
ROWS = OWN * COUNT
MESSAGE = ROWS + 1
TILE = 8
CHUNKS = 4
VMEM = pl.BlockSpec(memory_space=pltpu.VMEM)
ROOM = pltpu.CompilerParams(vmem_limit_bytes=8 << 20)
HBM = pl.BlockSpec(memory_space=pltpu.HBM)


def exchange(value):
    return lax.all_to_all(value, "grp", 0, 0, tiled=True, axis_index_groups=PLANES)


def in_hbm(value):
    return pltpu.with_memory_space_constraint(value, pltpu.HBM)


def thirds(value):
    high = value.astype(jnp.bfloat16)
    rest = value - high.astype(jnp.float32)
    mid = rest.astype(jnp.bfloat16)
    low = (rest - mid.astype(jnp.float32)).astype(jnp.bfloat16)
    return high, mid, low


def pack_kernel(table_hbm, coefs_hbm, grids_hbm, out_ref, table, coefs, grids, known_sem, grids_sem):
    known_copies = [
        pltpu.make_async_copy(table_hbm, table, known_sem.at[0]),
        pltpu.make_async_copy(coefs_hbm, coefs, known_sem.at[1]),
    ]
    chunk = FIELDS // CHUNKS
    spans = [pl.ds(i * chunk, chunk) for i in range(CHUNKS)]
    copies = [
        pltpu.make_async_copy(grids_hbm.at[:, span, :], grids.at[:, span, :], grids_sem.at[i])
        for i, span in enumerate(spans)
    ]
    for copy in known_copies + copies:
        copy.start()
    for copy in known_copies:
        copy.wait()
    slots = table.shape[1]
    lane = lax.broadcasted_iota(jnp.int32, (1, POINTS), 1) % COUNT
    labels = jnp.zeros((1, POINTS), jnp.int32)
    for i in range(COUNT):
        labels = jnp.where(lane == i, table[i // slots, i % slots], labels)
    labels = labels.astype(jnp.float32)
    row = lax.broadcasted_iota(jnp.int32, (COUNT, POINTS), 0)
    weight = jnp.zeros((COUNT, POINTS), jnp.int32)
    for g in range(COUNT // slots):
        weight = jnp.where(row // slots == g, coefs[g], weight)
    weight = weight.astype(jnp.float32)
    for peer in range(PEERS):
        out_ref[peer * MESSAGE + ROWS : (peer + 1) * MESSAGE, :] = labels
    for i, copy in enumerate(copies):
        copy.wait()
        for f in range(i * chunk, (i + 1) * chunk):
            peer, j = divmod(f, OWN)
            at = peer * MESSAGE + j * COUNT
            out_ref[at : at + COUNT, :] = grids[:, f, :] * weight


def in_one_row(rows):
    peer = lax.broadcasted_iota(jnp.int32, rows.shape, 0)
    part = lax.broadcasted_iota(jnp.int32, rows.shape, 1) // COUNT
    per = POINTS // COUNT
    return jnp.concatenate(
        [
            jnp.sum(jnp.where(peer == part + h * per, rows, 0.0), axis=0, keepdims=True)
            for h in range(PEERS // per)
        ],
        axis=1,
    )


def sum_kernel(got_ref, out_ref, labels_ref):
    labels = in_one_row(
        jnp.concatenate(
            [got_ref[(s + 1) * MESSAGE - 1 : (s + 1) * MESSAGE, :] for s in range(PEERS)], axis=0
        )
    )
    wanted = lax.broadcasted_iota(jnp.int32, (SUBS, PEERS * COUNT), 0).astype(jnp.float32)
    onehot = (labels == wanted).astype(jnp.float32).astype(jnp.bfloat16)

    def rows_of(s, j):
        at = s * MESSAGE + j * COUNT
        return got_ref[at : at + COUNT, :]

    data = jnp.concatenate(
        [
            jnp.concatenate([rows_of(s, j) for s in range(PEERS)], axis=0)
            for j in range(OWN)
        ],
        axis=1,
    )
    high, mid, low = (
        jnp.dot(onehot, part, preferred_element_type=jnp.float32) for part in thirds(data)
    )
    total = high + (mid + low)
    for j in range(OWN):
        out_ref[j] = total[:, j * POINTS : (j + 1) * POINTS]
    labels_ref[...] = jnp.broadcast_to(labels, labels_ref.shape)


def pick_kernel(pair_ref, other_pair_ref, labels_ref, out_ref):
    sparse = jnp.concatenate([pair_ref[j] + other_pair_ref[j] for j in range(OWN)], axis=1)
    wanted = lax.broadcasted_iota(jnp.int32, (SUBS, PEERS * COUNT), 0).astype(jnp.float32)
    onehot = (labels_ref[0:1, :] == wanted).astype(jnp.float32).T.astype(jnp.bfloat16)
    picks = jnp.dot(
        jnp.concatenate([onehot] * 3, axis=1),
        jnp.concatenate(thirds(sparse), axis=0),
        preferred_element_type=jnp.float32,
    )
    for j in range(OWN):
        out_ref[:, j * COUNT : (j + 1) * COUNT, :] = picks[
            :, j * POINTS : (j + 1) * POINTS
        ].reshape(PEERS, COUNT, POINTS)


def unpack_kernel(back_ref, out_hbm, held, sem):
    chunk = COUNT // CHUNKS
    copies = []
    for i in range(CHUNKS):
        for r in range(i * chunk, (i + 1) * chunk):
            for f in range(0, FIELDS, TILE):
                held[r, f : f + TILE, :] = back_ref[f : f + TILE, r, :]
        span = pl.ds(i * chunk, chunk)
        copies.append(pltpu.make_async_copy(held.at[span], out_hbm.at[span], sem.at[i]))
        copies[-1].start()
    for copy in copies:
        copy.wait()


def on_device(grids, table, coefs):
    f32 = jnp.float32
    messages = pl.pallas_call(
        pack_kernel,
        out_shape=jax.ShapeDtypeStruct((PEERS * MESSAGE, POINTS), f32),
        in_specs=[HBM, HBM, HBM],
        out_specs=VMEM,
        scratch_shapes=[
            pltpu.SMEM(table.shape, table.dtype),
            pltpu.SMEM(coefs.shape, coefs.dtype),
            pltpu.VMEM((COUNT, FIELDS, POINTS), f32),
            pltpu.SemaphoreType.DMA((2,)),
            pltpu.SemaphoreType.DMA((CHUNKS,)),
        ],
        compiler_params=ROOM,
    )(*map(in_hbm, (table, coefs, grids.reshape(COUNT, FIELDS, POINTS))))
    got = exchange(messages.reshape(PEERS, 1, MESSAGE * POINTS))
    partial, labels = pl.pallas_call(
        sum_kernel,
        out_shape=(
            jax.ShapeDtypeStruct((OWN, SUBS, POINTS), f32),
            jax.ShapeDtypeStruct((TILE, PEERS * COUNT), f32),
        ),
        in_specs=[VMEM],
        out_specs=(VMEM, VMEM),
        compiler_params=ROOM,
    )(got.reshape(PEERS * MESSAGE, POINTS))
    pair = partial + lax.ppermute(partial, "grp", partners(0))
    other_pair = lax.ppermute(pair, "grp", partners(1))
    picks = pl.pallas_call(
        pick_kernel,
        out_shape=jax.ShapeDtypeStruct((PEERS, ROWS, POINTS), f32),
        in_specs=[VMEM, VMEM, VMEM],
        out_specs=VMEM,
        compiler_params=ROOM,
    )(pair, other_pair, labels)
    back = exchange(picks).reshape(FIELDS, COUNT, POINTS)
    combined = pl.pallas_call(
        unpack_kernel,
        out_shape=jax.ShapeDtypeStruct((COUNT, FIELDS, POINTS), f32),
        in_specs=[VMEM],
        out_specs=HBM,
        scratch_shapes=[
            pltpu.VMEM((COUNT, FIELDS, POINTS), f32),
            pltpu.SemaphoreType.DMA((CHUNKS,)),
        ],
        compiler_params=ROOM,
    )(back)
    return combined.reshape(grids.shape)


def solution(mesh):
    return jax.shard_map(
        on_device,
        mesh=mesh,
        in_specs=(P("grp", None, None, "dom"), P("grp", None), P("grp")),
        out_specs=P("grp", None, None, "dom"),
        check_vma=False,
    )
```

```python
import jax
import jax.numpy as jnp
from jax import lax
from jax.experimental import pallas as pl
from jax.experimental.pallas import tpu as pltpu
from jax.sharding import PartitionSpec as P

SUBS = 64
Y, Z, CORES = 8, 4, 2
PLANES = [[(y * Z + z) * CORES + c for y in range(Y) for c in range(CORES)] for z in range(Z)]


def partners(turn):
    pairs = []
    for i in range(Y * Z * CORES):
        y, z, c = i // (Z * CORES), i // CORES % Z, i % CORES
        other = (Z - 1 - z, z ^ 1)[turn]
        pairs.append((i, (y * Z + other) * CORES + c))
    return pairs


PEERS = Y * CORES
COUNT = 16
FIELDS = 64
POINTS = 128
OWN = FIELDS // PEERS
ROWS = OWN * COUNT
MESSAGE = ROWS + 1
TILE = 8
CHUNKS = 4
VMEM = pl.BlockSpec(memory_space=pltpu.VMEM)
ROOM = pltpu.CompilerParams(vmem_limit_bytes=8 << 20)
HBM = pl.BlockSpec(memory_space=pltpu.HBM)


def exchange(value):
    return lax.all_to_all(value, "grp", 0, 0, tiled=True, axis_index_groups=PLANES)


def in_hbm(value):
    return pltpu.with_memory_space_constraint(value, pltpu.HBM)


def thirds(value):
    high = value.astype(jnp.bfloat16)
    rest = value - high.astype(jnp.float32)
    mid = rest.astype(jnp.bfloat16)
    low = (rest - mid.astype(jnp.float32)).astype(jnp.bfloat16)
    return high, mid, low


def pack_kernel(table_hbm, coefs_hbm, grids_hbm, out_ref, table, coefs, grids, known_sem, grids_sem):
    known_copies = [
        pltpu.make_async_copy(table_hbm, table, known_sem.at[0]),
        pltpu.make_async_copy(coefs_hbm, coefs, known_sem.at[1]),
    ]
    chunk = FIELDS // CHUNKS
    spans = [pl.ds(i * chunk, chunk) for i in range(CHUNKS)]
    copies = [
        pltpu.make_async_copy(grids_hbm.at[:, span, :], grids.at[:, span, :], grids_sem.at[i])
        for i, span in enumerate(spans)
    ]
    for copy in known_copies + copies:
        copy.start()
    for copy in known_copies:
        copy.wait()
    slots = table.shape[1]
    lane = lax.broadcasted_iota(jnp.int32, (1, POINTS), 1) % COUNT
    labels = jnp.zeros((1, POINTS), jnp.int32)
    for i in range(COUNT):
        labels = jnp.where(lane == i, table[i // slots, i % slots], labels)
    labels = labels.astype(jnp.float32)
    row = lax.broadcasted_iota(jnp.int32, (COUNT, POINTS), 0)
    weight = jnp.zeros((COUNT, POINTS), jnp.int32)
    for g in range(COUNT // slots):
        weight = jnp.where(row // slots == g, coefs[g], weight)
    weight = weight.astype(jnp.float32)
    for peer in range(PEERS):
        out_ref[peer * MESSAGE + ROWS : (peer + 1) * MESSAGE, :] = labels
    for i, copy in enumerate(copies):
        copy.wait()
        for f in range(i * chunk, (i + 1) * chunk):
            peer, j = divmod(f, OWN)
            at = peer * MESSAGE + j * COUNT
            out_ref[at : at + COUNT, :] = grids[:, f, :] * weight


def in_one_row(rows):
    peer = lax.broadcasted_iota(jnp.int32, rows.shape, 0)
    part = lax.broadcasted_iota(jnp.int32, rows.shape, 1) // COUNT
    per = POINTS // COUNT
    return jnp.concatenate(
        [
            jnp.sum(jnp.where(peer == part + h * per, rows, 0.0), axis=0, keepdims=True)
            for h in range(PEERS // per)
        ],
        axis=1,
    )


def sum_kernel(got_ref, out_ref, labels_ref):
    labels = in_one_row(
        jnp.concatenate(
            [got_ref[(s + 1) * MESSAGE - 1 : (s + 1) * MESSAGE, :] for s in range(PEERS)], axis=0
        )
    )
    wanted = lax.broadcasted_iota(jnp.int32, (SUBS, PEERS * COUNT), 0).astype(jnp.float32)
    onehot = (labels == wanted).astype(jnp.float32).astype(jnp.bfloat16)

    def rows_of(s, j):
        at = s * MESSAGE + j * COUNT
        return got_ref[at : at + COUNT, :]

    data = jnp.concatenate(
        [
            jnp.concatenate([rows_of(s, j) for s in range(PEERS)], axis=0)
            for j in range(OWN)
        ],
        axis=1,
    )
    high, mid, low = (
        jnp.dot(onehot, part, preferred_element_type=jnp.float32) for part in thirds(data)
    )
    total = high + (mid + low)
    for j in range(OWN):
        out_ref[j] = total[:, j * POINTS : (j + 1) * POINTS]
    labels_ref[...] = jnp.broadcast_to(labels, labels_ref.shape)


def pick_kernel(pair_ref, other_pair_ref, labels_ref, out_ref):
    sparse = jnp.concatenate([pair_ref[j] + other_pair_ref[j] for j in range(OWN)], axis=1)
    wanted = lax.broadcasted_iota(jnp.int32, (SUBS, PEERS * COUNT), 0).astype(jnp.float32)
    onehot = (labels_ref[0:1, :] == wanted).astype(jnp.float32).T.astype(jnp.bfloat16)
    picks = jnp.dot(
        jnp.concatenate([onehot] * 3, axis=1),
        jnp.concatenate(thirds(sparse), axis=0),
        preferred_element_type=jnp.float32,
    )
    for j in range(OWN):
        out_ref[:, j * COUNT : (j + 1) * COUNT, :] = picks[
            :, j * POINTS : (j + 1) * POINTS
        ].reshape(PEERS, COUNT, POINTS)


def unpack_kernel(back_ref, out_hbm, held, sem):
    chunk = COUNT // CHUNKS
    copies = []
    for i in range(CHUNKS):
        for r in range(i * chunk, (i + 1) * chunk):
            for f in range(0, FIELDS, TILE):
                held[r, f : f + TILE, :] = back_ref[f : f + TILE, r, :]
        span = pl.ds(i * chunk, chunk)
        copies.append(pltpu.make_async_copy(held.at[span], out_hbm.at[span], sem.at[i]))
        copies[-1].start()
    for copy in copies:
        copy.wait()


def on_device(grids, table, coefs):
    f32 = jnp.float32
    messages = pl.pallas_call(
        pack_kernel,
        out_shape=jax.ShapeDtypeStruct((PEERS * MESSAGE, POINTS), f32),
        in_specs=[HBM, HBM, HBM],
        out_specs=VMEM,
        scratch_shapes=[
            pltpu.SMEM(table.shape, table.dtype),
            pltpu.SMEM(coefs.shape, coefs.dtype),
            pltpu.VMEM((COUNT, FIELDS, POINTS), f32),
            pltpu.SemaphoreType.DMA((2,)),
            pltpu.SemaphoreType.DMA((CHUNKS,)),
        ],
        compiler_params=ROOM,
    )(*map(in_hbm, (table, coefs, grids.reshape(COUNT, FIELDS, POINTS))))
    got = exchange(messages.reshape(PEERS, 1, MESSAGE * POINTS))
    partial, labels = pl.pallas_call(
        sum_kernel,
        out_shape=(
            jax.ShapeDtypeStruct((OWN, SUBS, POINTS), f32),
            jax.ShapeDtypeStruct((TILE, PEERS * COUNT), f32),
        ),
        in_specs=[VMEM],
        out_specs=(VMEM, VMEM),
        compiler_params=ROOM,
    )(got.reshape(PEERS * MESSAGE, POINTS))
    pair = partial + lax.ppermute(partial, "grp", partners(0))
    other_pair = lax.ppermute(pair, "grp", partners(1))
    picks = pl.pallas_call(
        pick_kernel,
        out_shape=jax.ShapeDtypeStruct((PEERS, ROWS, POINTS), f32),
        in_specs=[VMEM, VMEM, VMEM],
        out_specs=VMEM,
        compiler_params=ROOM,
    )(pair, other_pair, labels)
    back = exchange(picks).reshape(FIELDS, COUNT, POINTS)
    combined = pl.pallas_call(
        unpack_kernel,
        out_shape=jax.ShapeDtypeStruct((COUNT, FIELDS, POINTS), f32),
        in_specs=[VMEM],
        out_specs=HBM,
        scratch_shapes=[
            pltpu.VMEM((COUNT, FIELDS, POINTS), f32),
            pltpu.SemaphoreType.DMA((CHUNKS,)),
        ],
        compiler_params=ROOM,
    )(back)
    return combined.reshape(grids.shape)


def solution(mesh):
    return jax.shard_map(
        on_device,
        mesh=mesh,
        in_specs=(P("grp", None, None, "dom"), P("grp", None), P("grp")),
        out_specs=P("grp", None, None, "dom"),
        check_vma=False,
    )
```

```python
import jax
import jax.numpy as jnp
from jax import lax
from jax.experimental import pallas as pl
from jax.experimental.pallas import tpu as pltpu
from jax.sharding import PartitionSpec as P

SUBS = 64
Y, Z, CORES = 8, 4, 2
PLANES = [[(y * Z + z) * CORES + c for y in range(Y) for c in range(CORES)] for z in range(Z)]


def partners(turn):
    pairs = []
    for i in range(Y * Z * CORES):
        y, z, c = i // (Z * CORES), i // CORES % Z, i % CORES
        other = z ^ 1 if turn != c else Z - 1 - z
        pairs.append((i, (y * Z + other) * CORES + c))
    return pairs


PEERS = Y * CORES
COUNT = 16
FIELDS = 64
POINTS = 128
OWN = FIELDS // PEERS
ROWS = OWN * COUNT
MESSAGE = ROWS + 1
TILE = 8
CHUNKS = 4
VMEM = pl.BlockSpec(memory_space=pltpu.VMEM)
ROOM = pltpu.CompilerParams(vmem_limit_bytes=8 << 20)
HBM = pl.BlockSpec(memory_space=pltpu.HBM)


def exchange(value):
    return lax.all_to_all(value, "grp", 0, 0, tiled=True, axis_index_groups=PLANES)


def in_hbm(value):
    return pltpu.with_memory_space_constraint(value, pltpu.HBM)


def thirds(value):
    high = value.astype(jnp.bfloat16)
    rest = value - high.astype(jnp.float32)
    mid = rest.astype(jnp.bfloat16)
    low = (rest - mid.astype(jnp.float32)).astype(jnp.bfloat16)
    return high, mid, low


def pack_kernel(table_hbm, coefs_hbm, grids_hbm, out_ref, table, coefs, grids, known_sem, grids_sem):
    known_copies = [
        pltpu.make_async_copy(table_hbm, table, known_sem.at[0]),
        pltpu.make_async_copy(coefs_hbm, coefs, known_sem.at[1]),
    ]
    chunk = FIELDS // CHUNKS
    spans = [pl.ds(i * chunk, chunk) for i in range(CHUNKS)]
    copies = [
        pltpu.make_async_copy(grids_hbm.at[:, span, :], grids.at[:, span, :], grids_sem.at[i])
        for i, span in enumerate(spans)
    ]
    for copy in known_copies + copies:
        copy.start()
    for copy in known_copies:
        copy.wait()
    slots = table.shape[1]
    lane = lax.broadcasted_iota(jnp.int32, (1, POINTS), 1) % COUNT
    labels = jnp.zeros((1, POINTS), jnp.int32)
    for i in range(COUNT):
        labels = jnp.where(lane == i, table[i // slots, i % slots], labels)
    labels = labels.astype(jnp.float32)
    row = lax.broadcasted_iota(jnp.int32, (COUNT, POINTS), 0)
    weight = jnp.zeros((COUNT, POINTS), jnp.int32)
    for g in range(COUNT // slots):
        weight = jnp.where(row // slots == g, coefs[g], weight)
    weight = weight.astype(jnp.float32)
    for peer in range(PEERS):
        out_ref[peer * MESSAGE + ROWS : (peer + 1) * MESSAGE, :] = labels
    for i, copy in enumerate(copies):
        copy.wait()
        for f in range(i * chunk, (i + 1) * chunk):
            peer, j = divmod(f, OWN)
            at = peer * MESSAGE + j * COUNT
            out_ref[at : at + COUNT, :] = grids[:, f, :] * weight


def in_one_row(rows):
    peer = lax.broadcasted_iota(jnp.int32, rows.shape, 0)
    part = lax.broadcasted_iota(jnp.int32, rows.shape, 1) // COUNT
    per = POINTS // COUNT
    return jnp.concatenate(
        [
            jnp.sum(jnp.where(peer == part + h * per, rows, 0.0), axis=0, keepdims=True)
            for h in range(PEERS // per)
        ],
        axis=1,
    )


def sum_kernel(got_ref, out_ref, labels_ref):
    labels = in_one_row(
        jnp.concatenate(
            [got_ref[(s + 1) * MESSAGE - 1 : (s + 1) * MESSAGE, :] for s in range(PEERS)], axis=0
        )
    )
    wanted = lax.broadcasted_iota(jnp.int32, (SUBS, PEERS * COUNT), 0).astype(jnp.float32)
    onehot = (labels == wanted).astype(jnp.float32).astype(jnp.bfloat16)

    def rows_of(s, j):
        at = s * MESSAGE + j * COUNT
        return got_ref[at : at + COUNT, :]

    data = jnp.concatenate(
        [
            jnp.concatenate([rows_of(s, j) for s in range(PEERS)], axis=0)
            for j in range(OWN)
        ],
        axis=1,
    )
    high, mid, low = (
        jnp.dot(onehot, part, preferred_element_type=jnp.float32) for part in thirds(data)
    )
    total = high + (mid + low)
    for j in range(OWN):
        out_ref[j] = total[:, j * POINTS : (j + 1) * POINTS]
    labels_ref[...] = jnp.broadcast_to(labels, labels_ref.shape)


def pick_kernel(pair_ref, other_pair_ref, labels_ref, out_ref):
    sparse = jnp.concatenate([pair_ref[j] + other_pair_ref[j] for j in range(OWN)], axis=1)
    wanted = lax.broadcasted_iota(jnp.int32, (SUBS, PEERS * COUNT), 0).astype(jnp.float32)
    onehot = (labels_ref[0:1, :] == wanted).astype(jnp.float32).T.astype(jnp.bfloat16)
    picks = jnp.dot(
        jnp.concatenate([onehot] * 3, axis=1),
        jnp.concatenate(thirds(sparse), axis=0),
        preferred_element_type=jnp.float32,
    )
    for j in range(OWN):
        out_ref[:, j * COUNT : (j + 1) * COUNT, :] = picks[
            :, j * POINTS : (j + 1) * POINTS
        ].reshape(PEERS, COUNT, POINTS)


def unpack_kernel(back_ref, out_hbm, held, sem):
    chunk = COUNT // CHUNKS
    copies = []
    for i in range(CHUNKS):
        for r in range(i * chunk, (i + 1) * chunk):
            for f in range(0, FIELDS, TILE):
                held[r, f : f + TILE, :] = back_ref[f : f + TILE, r, :]
        span = pl.ds(i * chunk, chunk)
        copies.append(pltpu.make_async_copy(held.at[span], out_hbm.at[span], sem.at[i]))
        copies[-1].start()
    for copy in copies:
        copy.wait()


def on_device(grids, table, coefs):
    f32 = jnp.float32
    messages = pl.pallas_call(
        pack_kernel,
        out_shape=jax.ShapeDtypeStruct((PEERS * MESSAGE, POINTS), f32),
        in_specs=[HBM, HBM, HBM],
        out_specs=VMEM,
        scratch_shapes=[
            pltpu.SMEM(table.shape, table.dtype),
            pltpu.SMEM(coefs.shape, coefs.dtype),
            pltpu.VMEM((COUNT, FIELDS, POINTS), f32),
            pltpu.SemaphoreType.DMA((2,)),
            pltpu.SemaphoreType.DMA((CHUNKS,)),
        ],
        compiler_params=ROOM,
    )(*map(in_hbm, (table, coefs, grids.reshape(COUNT, FIELDS, POINTS))))
    got = exchange(messages.reshape(PEERS, 1, MESSAGE * POINTS))
    partial, labels = pl.pallas_call(
        sum_kernel,
        out_shape=(
            jax.ShapeDtypeStruct((OWN, SUBS, POINTS), f32),
            jax.ShapeDtypeStruct((TILE, PEERS * COUNT), f32),
        ),
        in_specs=[VMEM],
        out_specs=(VMEM, VMEM),
        compiler_params=ROOM,
    )(got.reshape(PEERS * MESSAGE, POINTS))
    pair = partial + lax.ppermute(partial, "grp", partners(0))
    other_pair = lax.ppermute(pair, "grp", partners(1))
    picks = pl.pallas_call(
        pick_kernel,
        out_shape=jax.ShapeDtypeStruct((PEERS, ROWS, POINTS), f32),
        in_specs=[VMEM, VMEM, VMEM],
        out_specs=VMEM,
        compiler_params=ROOM,
    )(pair, other_pair, labels)
    back = exchange(picks).reshape(FIELDS, COUNT, POINTS)
    combined = pl.pallas_call(
        unpack_kernel,
        out_shape=jax.ShapeDtypeStruct((COUNT, FIELDS, POINTS), f32),
        in_specs=[VMEM],
        out_specs=HBM,
        scratch_shapes=[
            pltpu.VMEM((COUNT, FIELDS, POINTS), f32),
            pltpu.SemaphoreType.DMA((CHUNKS,)),
        ],
        compiler_params=ROOM,
    )(back)
    return combined.reshape(grids.shape)


def solution(mesh):
    return jax.shard_map(
        on_device,
        mesh=mesh,
        in_specs=(P("grp", None, None, "dom"), P("grp", None), P("grp")),
        out_specs=P("grp", None, None, "dom"),
        check_vma=False,
    )
```

```python
import jax
import jax.numpy as jnp
from jax import lax
from jax.experimental import pallas as pl
from jax.experimental.pallas import tpu as pltpu
from jax.sharding import PartitionSpec as P

SUBS = 64
Y, Z, CORES = 8, 4, 2
PLANES = [[(y * Z + z) * CORES + c for y in range(Y) for c in range(CORES)] for z in range(Z)]
COLUMNS = [
    [(y * Z + (Z - 1 - z if c else z)) * CORES + c for z in range(Z)]
    for y in range(Y)
    for c in range(CORES)
]
PEERS = Y * CORES
COUNT = 16
FIELDS = 64
POINTS = 128
OWN = FIELDS // PEERS
ROWS = OWN * COUNT
MESSAGE = ROWS + 1
TILE = 8
CHUNKS = 4
VMEM = pl.BlockSpec(memory_space=pltpu.VMEM)
ROOM = pltpu.CompilerParams(vmem_limit_bytes=8 << 20)
HBM = pl.BlockSpec(memory_space=pltpu.HBM)


def exchange(value):
    return lax.all_to_all(value, "grp", 0, 0, tiled=True, axis_index_groups=PLANES)


def in_hbm(value):
    return pltpu.with_memory_space_constraint(value, pltpu.HBM)


def thirds(value):
    high = value.astype(jnp.bfloat16)
    rest = value - high.astype(jnp.float32)
    mid = rest.astype(jnp.bfloat16)
    low = (rest - mid.astype(jnp.float32)).astype(jnp.bfloat16)
    return high, mid, low


def pack_kernel(table_hbm, coefs_hbm, grids_hbm, out_ref, table, coefs, grids, known_sem, grids_sem):
    known_copies = [
        pltpu.make_async_copy(table_hbm, table, known_sem.at[0]),
        pltpu.make_async_copy(coefs_hbm, coefs, known_sem.at[1]),
    ]
    chunk = FIELDS // CHUNKS
    spans = [pl.ds(i * chunk, chunk) for i in range(CHUNKS)]
    copies = [
        pltpu.make_async_copy(grids_hbm.at[:, span, :], grids.at[:, span, :], grids_sem.at[i])
        for i, span in enumerate(spans)
    ]
    for copy in known_copies + copies:
        copy.start()
    for copy in known_copies:
        copy.wait()
    slots = table.shape[1]
    lane = lax.broadcasted_iota(jnp.int32, (1, POINTS), 1) % COUNT
    labels = jnp.zeros((1, POINTS), jnp.int32)
    for i in range(COUNT):
        labels = jnp.where(lane == i, table[i // slots, i % slots], labels)
    labels = labels.astype(jnp.float32)
    row = lax.broadcasted_iota(jnp.int32, (COUNT, POINTS), 0)
    weight = jnp.zeros((COUNT, POINTS), jnp.int32)
    for g in range(COUNT // slots):
        weight = jnp.where(row // slots == g, coefs[g], weight)
    weight = weight.astype(jnp.float32)
    for peer in range(PEERS):
        out_ref[peer * MESSAGE + ROWS : (peer + 1) * MESSAGE, :] = labels
    for i, copy in enumerate(copies):
        copy.wait()
        for f in range(i * chunk, (i + 1) * chunk):
            peer, j = divmod(f, OWN)
            at = peer * MESSAGE + j * COUNT
            out_ref[at : at + COUNT, :] = grids[:, f, :] * weight


def in_one_row(rows):
    peer = lax.broadcasted_iota(jnp.int32, rows.shape, 0)
    part = lax.broadcasted_iota(jnp.int32, rows.shape, 1) // COUNT
    per = POINTS // COUNT
    return jnp.concatenate(
        [
            jnp.sum(jnp.where(peer == part + h * per, rows, 0.0), axis=0, keepdims=True)
            for h in range(PEERS // per)
        ],
        axis=1,
    )


def sum_kernel(got_ref, out_ref, labels_ref):
    labels = in_one_row(
        jnp.concatenate(
            [got_ref[(s + 1) * MESSAGE - 1 : (s + 1) * MESSAGE, :] for s in range(PEERS)], axis=0
        )
    )
    wanted = lax.broadcasted_iota(jnp.int32, (SUBS, PEERS * COUNT), 0).astype(jnp.float32)
    onehot = (labels == wanted).astype(jnp.float32).astype(jnp.bfloat16)

    def rows_of(s, j):
        at = s * MESSAGE + j * COUNT
        return got_ref[at : at + COUNT, :]

    data = jnp.concatenate(
        [
            jnp.concatenate([rows_of(s, j) for s in range(PEERS)], axis=0)
            for j in range(OWN)
        ],
        axis=1,
    )
    high, mid, low = (
        jnp.dot(onehot, part, preferred_element_type=jnp.float32) for part in thirds(data)
    )
    total = high + (mid + low)
    for j in range(OWN):
        out_ref[j] = total[:, j * POINTS : (j + 1) * POINTS]
    labels_ref[...] = jnp.broadcast_to(labels, labels_ref.shape)


def pick_kernel(every_ref, labels_ref, out_ref):
    sparse = jnp.concatenate(
        [
            (every_ref[0, j] + every_ref[1, j]) + (every_ref[2, j] + every_ref[3, j])
            for j in range(OWN)
        ],
        axis=1,
    )
    wanted = lax.broadcasted_iota(jnp.int32, (SUBS, PEERS * COUNT), 0).astype(jnp.float32)
    onehot = (labels_ref[0:1, :] == wanted).astype(jnp.float32).T.astype(jnp.bfloat16)
    picks = jnp.dot(
        jnp.concatenate([onehot] * 3, axis=1),
        jnp.concatenate(thirds(sparse), axis=0),
        preferred_element_type=jnp.float32,
    )
    for j in range(OWN):
        out_ref[:, j * COUNT : (j + 1) * COUNT, :] = picks[
            :, j * POINTS : (j + 1) * POINTS
        ].reshape(PEERS, COUNT, POINTS)


def unpack_kernel(back_ref, out_hbm, held, sem):
    chunk = COUNT // CHUNKS
    copies = []
    for i in range(CHUNKS):
        for r in range(i * chunk, (i + 1) * chunk):
            for f in range(0, FIELDS, TILE):
                held[r, f : f + TILE, :] = back_ref[f : f + TILE, r, :]
        span = pl.ds(i * chunk, chunk)
        copies.append(pltpu.make_async_copy(held.at[span], out_hbm.at[span], sem.at[i]))
        copies[-1].start()
    for copy in copies:
        copy.wait()


def on_device(grids, table, coefs):
    f32 = jnp.float32
    messages = pl.pallas_call(
        pack_kernel,
        out_shape=jax.ShapeDtypeStruct((PEERS * MESSAGE, POINTS), f32),
        in_specs=[HBM, HBM, HBM],
        out_specs=VMEM,
        scratch_shapes=[
            pltpu.SMEM(table.shape, table.dtype),
            pltpu.SMEM(coefs.shape, coefs.dtype),
            pltpu.VMEM((COUNT, FIELDS, POINTS), f32),
            pltpu.SemaphoreType.DMA((2,)),
            pltpu.SemaphoreType.DMA((CHUNKS,)),
        ],
        compiler_params=ROOM,
    )(*map(in_hbm, (table, coefs, grids.reshape(COUNT, FIELDS, POINTS))))
    got = exchange(messages.reshape(PEERS, 1, MESSAGE * POINTS))
    partial, labels = pl.pallas_call(
        sum_kernel,
        out_shape=(
            jax.ShapeDtypeStruct((OWN, SUBS, POINTS), f32),
            jax.ShapeDtypeStruct((TILE, PEERS * COUNT), f32),
        ),
        in_specs=[VMEM],
        out_specs=(VMEM, VMEM),
        compiler_params=ROOM,
    )(got.reshape(PEERS * MESSAGE, POINTS))
    every = lax.all_gather(partial, "grp", axis_index_groups=COLUMNS)
    picks = pl.pallas_call(
        pick_kernel,
        out_shape=jax.ShapeDtypeStruct((PEERS, ROWS, POINTS), f32),
        in_specs=[VMEM, VMEM],
        out_specs=VMEM,
        compiler_params=ROOM,
    )(every, labels)
    back = exchange(picks).reshape(FIELDS, COUNT, POINTS)
    combined = pl.pallas_call(
        unpack_kernel,
        out_shape=jax.ShapeDtypeStruct((COUNT, FIELDS, POINTS), f32),
        in_specs=[VMEM],
        out_specs=HBM,
        scratch_shapes=[
            pltpu.VMEM((COUNT, FIELDS, POINTS), f32),
            pltpu.SemaphoreType.DMA((CHUNKS,)),
        ],
        compiler_params=ROOM,
    )(back)
    return combined.reshape(grids.shape)


def solution(mesh):
    return jax.shard_map(
        on_device,
        mesh=mesh,
        in_specs=(P("grp", None, None, "dom"), P("grp", None), P("grp")),
        out_specs=P("grp", None, None, "dom"),
        check_vma=False,
    )
```

```python
import jax
import jax.numpy as jnp
from jax import lax
from jax.experimental import pallas as pl
from jax.experimental.pallas import tpu as pltpu
from jax.sharding import PartitionSpec as P

SUBS = 64
Y, Z, CORES = 8, 4, 2
PLANES = [[(y * Z + z) * CORES + c for y in range(Y) for c in range(CORES)] for z in range(Z)]


X, Z_LOW = 4, 3


def partners(turn):
    pairs = []
    for i in range(Y * Z * CORES):
        y, z, c = i // (Z * CORES), i // CORES % Z, i % CORES
        for dom in range(X * Z_LOW):
            first = c if dom % Z_LOW else 1 - c
            other = z ^ 1 if turn == first else Z - 1 - z
            pairs.append((i * X * Z_LOW + dom, ((y * Z + other) * CORES + c) * X * Z_LOW + dom))
    return pairs


PEERS = Y * CORES
COUNT = 16
FIELDS = 64
POINTS = 128
OWN = FIELDS // PEERS
ROWS = OWN * COUNT
MESSAGE = ROWS + 1
TILE = 8
CHUNKS = 4
HALVES = 2
VMEM = pl.BlockSpec(memory_space=pltpu.VMEM)
ROOM = pltpu.CompilerParams(vmem_limit_bytes=8 << 20)
HBM = pl.BlockSpec(memory_space=pltpu.HBM)


def exchange(value):
    return lax.all_to_all(value, "grp", 0, 0, tiled=True, axis_index_groups=PLANES)


def in_hbm(value):
    return pltpu.with_memory_space_constraint(value, pltpu.HBM)


def thirds(value):
    high = value.astype(jnp.bfloat16)
    rest = value - high.astype(jnp.float32)
    mid = rest.astype(jnp.bfloat16)
    low = (rest - mid.astype(jnp.float32)).astype(jnp.bfloat16)
    return high, mid, low


def pack_kernel(table_hbm, coefs_hbm, grids_hbm, out_ref, table, coefs, grids, known_sem, grids_sem):
    known_copies = [
        pltpu.make_async_copy(table_hbm, table, known_sem.at[0]),
        pltpu.make_async_copy(coefs_hbm, coefs, known_sem.at[1]),
    ]
    chunk = FIELDS // CHUNKS
    spans = [pl.ds(i * chunk, chunk) for i in range(CHUNKS)]
    copies = [
        pltpu.make_async_copy(grids_hbm.at[:, span, :], grids.at[:, span, :], grids_sem.at[i])
        for i, span in enumerate(spans)
    ]
    for copy in known_copies + copies:
        copy.start()
    for copy in known_copies:
        copy.wait()
    slots = table.shape[1]
    lane = lax.broadcasted_iota(jnp.int32, (1, POINTS), 1) % COUNT
    labels = jnp.zeros((1, POINTS), jnp.int32)
    for i in range(COUNT):
        labels = jnp.where(lane == i, table[i // slots, i % slots], labels)
    labels = labels.astype(jnp.float32)
    row = lax.broadcasted_iota(jnp.int32, (COUNT, POINTS), 0)
    weight = jnp.zeros((COUNT, POINTS), jnp.int32)
    for g in range(COUNT // slots):
        weight = jnp.where(row // slots == g, coefs[g], weight)
    weight = weight.astype(jnp.float32)
    for peer in range(PEERS):
        out_ref[peer * MESSAGE + ROWS : (peer + 1) * MESSAGE, :] = labels
    for i, copy in enumerate(copies):
        copy.wait()
        for f in range(i * chunk, (i + 1) * chunk):
            peer, j = divmod(f, OWN)
            at = peer * MESSAGE + j * COUNT
            out_ref[at : at + COUNT, :] = grids[:, f, :] * weight


def in_one_row(rows):
    peer = lax.broadcasted_iota(jnp.int32, rows.shape, 0)
    part = lax.broadcasted_iota(jnp.int32, rows.shape, 1) // COUNT
    per = POINTS // COUNT
    return jnp.concatenate(
        [
            jnp.sum(jnp.where(peer == part + h * per, rows, 0.0), axis=0, keepdims=True)
            for h in range(PEERS // per)
        ],
        axis=1,
    )


def sum_kernel(got_ref, out_ref, labels_ref):
    labels = in_one_row(
        jnp.concatenate(
            [got_ref[(s + 1) * MESSAGE - 1 : (s + 1) * MESSAGE, :] for s in range(PEERS)], axis=0
        )
    )
    wanted = lax.broadcasted_iota(jnp.int32, (SUBS, PEERS * COUNT), 0).astype(jnp.float32)
    onehot = (labels == wanted).astype(jnp.float32).astype(jnp.bfloat16)

    def rows_of(s, j):
        at = s * MESSAGE + j * COUNT
        return got_ref[at : at + COUNT, :]

    data = jnp.concatenate(
        [
            jnp.concatenate([rows_of(s, j) for s in range(PEERS)], axis=0)
            for j in range(OWN)
        ],
        axis=1,
    )
    high, mid, low = (
        jnp.dot(onehot, part, preferred_element_type=jnp.float32) for part in thirds(data)
    )
    total = high + (mid + low)
    for j in range(OWN):
        out_ref[j] = total[:, j * POINTS : (j + 1) * POINTS]
    labels_ref[...] = jnp.broadcast_to(labels, labels_ref.shape)


def pick_kernel(pair_ref, other_pair_ref, labels_ref, out_ref):
    sparse = jnp.concatenate([pair_ref[j] + other_pair_ref[j] for j in range(OWN)], axis=1)
    wanted = lax.broadcasted_iota(jnp.int32, (SUBS, PEERS * COUNT), 0).astype(jnp.float32)
    onehot = (labels_ref[0:1, :] == wanted).astype(jnp.float32).T.astype(jnp.bfloat16)
    picks = jnp.dot(
        jnp.concatenate([onehot] * 3, axis=1),
        jnp.concatenate(thirds(sparse), axis=0),
        preferred_element_type=jnp.float32,
    )
    for j in range(OWN):
        out_ref[:, j * COUNT : (j + 1) * COUNT, :] = picks[
            :, j * POINTS : (j + 1) * POINTS
        ].reshape(PEERS, COUNT, POINTS)


def unpack_kernel(back_ref, out_hbm, held, sem):
    direct = COUNT // 2
    chunk = (COUNT - direct) // HALVES
    copies = [
        pltpu.make_async_copy(back_ref.at[:, r, :], out_hbm.at[r], sem.at[r])
        for r in range(direct)
    ]
    for copy in copies:
        copy.start()
    for i in range(HALVES):
        for r in range(i * chunk, (i + 1) * chunk):
            for f in range(0, FIELDS, TILE):
                held[r, f : f + TILE, :] = back_ref[f : f + TILE, direct + r, :]
        copies.append(
            pltpu.make_async_copy(
                held.at[pl.ds(i * chunk, chunk)],
                out_hbm.at[pl.ds(direct + i * chunk, chunk)],
                sem.at[direct + i],
            )
        )
        copies[-1].start()
    for copy in copies:
        copy.wait()


def on_device(grids, table, coefs):
    f32 = jnp.float32
    messages = pl.pallas_call(
        pack_kernel,
        out_shape=jax.ShapeDtypeStruct((PEERS * MESSAGE, POINTS), f32),
        in_specs=[HBM, HBM, HBM],
        out_specs=VMEM,
        scratch_shapes=[
            pltpu.SMEM(table.shape, table.dtype),
            pltpu.SMEM(coefs.shape, coefs.dtype),
            pltpu.VMEM((COUNT, FIELDS, POINTS), f32),
            pltpu.SemaphoreType.DMA((2,)),
            pltpu.SemaphoreType.DMA((CHUNKS,)),
        ],
        compiler_params=ROOM,
    )(*map(in_hbm, (table, coefs, grids.reshape(COUNT, FIELDS, POINTS))))
    got = exchange(messages.reshape(PEERS, 1, MESSAGE * POINTS))
    partial, labels = pl.pallas_call(
        sum_kernel,
        out_shape=(
            jax.ShapeDtypeStruct((OWN, SUBS, POINTS), f32),
            jax.ShapeDtypeStruct((TILE, PEERS * COUNT), f32),
        ),
        in_specs=[VMEM],
        out_specs=(VMEM, VMEM),
        compiler_params=ROOM,
    )(got.reshape(PEERS * MESSAGE, POINTS))
    pair = partial + lax.ppermute(partial, ("grp", "dom"), partners(0))
    other_pair = lax.ppermute(pair, ("grp", "dom"), partners(1))
    picks = pl.pallas_call(
        pick_kernel,
        out_shape=jax.ShapeDtypeStruct((PEERS, ROWS, POINTS), f32),
        in_specs=[VMEM, VMEM, VMEM],
        out_specs=VMEM,
        compiler_params=ROOM,
    )(pair, other_pair, labels)
    back = exchange(picks).reshape(FIELDS, COUNT, POINTS)
    combined = pl.pallas_call(
        unpack_kernel,
        out_shape=jax.ShapeDtypeStruct((COUNT, FIELDS, POINTS), f32),
        in_specs=[VMEM],
        out_specs=HBM,
        scratch_shapes=[
            pltpu.VMEM((COUNT // 2, FIELDS, POINTS), f32),
            pltpu.SemaphoreType.DMA((COUNT // 2 + HALVES,)),
        ],
        compiler_params=ROOM,
    )(back)
    return combined.reshape(grids.shape)


def solution(mesh):
    return jax.shard_map(
        on_device,
        mesh=mesh,
        in_specs=(P("grp", None, None, "dom"), P("grp", None), P("grp")),
        out_specs=P("grp", None, None, "dom"),
        check_vma=False,
    )
```

```python
import jax
import jax.numpy as jnp
from jax import lax
from jax.experimental import pallas as pl
from jax.experimental.pallas import tpu as pltpu
from jax.sharding import Mesh
from jax.sharding import PartitionSpec as P

SUBS = 64
Y, Z, CORES = 8, 4, 2
PEERS = Y * CORES
COUNT = 16
FIELDS = 64
POINTS = 128
OWN = FIELDS // PEERS
ROWS = OWN * COUNT
MESSAGE = ROWS + 1
TILE = 8
CHUNKS = 4
VMEM = pl.BlockSpec(memory_space=pltpu.VMEM)
ROOM = pltpu.CompilerParams(vmem_limit_bytes=8 << 20)
HBM = pl.BlockSpec(memory_space=pltpu.HBM)


def exchange(value):
    return lax.all_to_all(value, ("y", "core"), 0, 0, tiled=True)


def in_hbm(value):
    return pltpu.with_memory_space_constraint(value, pltpu.HBM)


def thirds(value):
    high = value.astype(jnp.bfloat16)
    rest = value - high.astype(jnp.float32)
    mid = rest.astype(jnp.bfloat16)
    low = (rest - mid.astype(jnp.float32)).astype(jnp.bfloat16)
    return high, mid, low


def pack_kernel(table_hbm, coefs_hbm, grids_hbm, out_ref, table, coefs, grids, known_sem, grids_sem):
    known_copies = [
        pltpu.make_async_copy(table_hbm, table, known_sem.at[0]),
        pltpu.make_async_copy(coefs_hbm, coefs, known_sem.at[1]),
    ]
    chunk = FIELDS // CHUNKS
    spans = [pl.ds(i * chunk, chunk) for i in range(CHUNKS)]
    copies = [
        pltpu.make_async_copy(grids_hbm.at[:, span, :], grids.at[:, span, :], grids_sem.at[i])
        for i, span in enumerate(spans)
    ]
    for copy in known_copies + copies:
        copy.start()
    for copy in known_copies:
        copy.wait()
    slots = table.shape[1]
    lane = lax.broadcasted_iota(jnp.int32, (1, POINTS), 1) % COUNT
    labels = jnp.zeros((1, POINTS), jnp.int32)
    for i in range(COUNT):
        labels = jnp.where(lane == i, table[i // slots, i % slots], labels)
    labels = labels.astype(jnp.float32)
    row = lax.broadcasted_iota(jnp.int32, (COUNT, POINTS), 0)
    weight = jnp.zeros((COUNT, POINTS), jnp.int32)
    for g in range(COUNT // slots):
        weight = jnp.where(row // slots == g, coefs[g], weight)
    weight = weight.astype(jnp.float32)
    for peer in range(PEERS):
        out_ref[peer * MESSAGE + ROWS : (peer + 1) * MESSAGE, :] = labels
    for i, copy in enumerate(copies):
        copy.wait()
        for f in range(i * chunk, (i + 1) * chunk):
            peer, j = divmod(f, OWN)
            at = peer * MESSAGE + j * COUNT
            out_ref[at : at + COUNT, :] = grids[:, f, :] * weight


def in_one_row(rows):
    peer = lax.broadcasted_iota(jnp.int32, rows.shape, 0)
    part = lax.broadcasted_iota(jnp.int32, rows.shape, 1) // COUNT
    per = POINTS // COUNT
    return jnp.concatenate(
        [
            jnp.sum(jnp.where(peer == part + h * per, rows, 0.0), axis=0, keepdims=True)
            for h in range(PEERS // per)
        ],
        axis=1,
    )


def sum_kernel(got_ref, out_ref, labels_ref):
    labels = in_one_row(
        jnp.concatenate(
            [got_ref[(s + 1) * MESSAGE - 1 : (s + 1) * MESSAGE, :] for s in range(PEERS)], axis=0
        )
    )
    wanted = lax.broadcasted_iota(jnp.int32, (SUBS, PEERS * COUNT), 0).astype(jnp.float32)
    onehot = (labels == wanted).astype(jnp.float32).astype(jnp.bfloat16)

    def rows_of(s, j):
        at = s * MESSAGE + j * COUNT
        return got_ref[at : at + COUNT, :]

    data = jnp.concatenate(
        [
            jnp.concatenate([rows_of(s, j) for s in range(PEERS)], axis=0)
            for j in range(OWN)
        ],
        axis=1,
    )
    high, mid, low = (
        jnp.dot(onehot, part, preferred_element_type=jnp.float32) for part in thirds(data)
    )
    total = high + (mid + low)
    for j in range(OWN):
        out_ref[j] = total[:, j * POINTS : (j + 1) * POINTS]
    labels_ref[...] = jnp.broadcast_to(labels, labels_ref.shape)


def pick_kernel(every_ref, labels_ref, out_ref):
    sparse = jnp.concatenate(
        [
            (every_ref[0, j] + every_ref[1, j]) + (every_ref[2, j] + every_ref[3, j])
            for j in range(OWN)
        ],
        axis=1,
    )
    wanted = lax.broadcasted_iota(jnp.int32, (SUBS, PEERS * COUNT), 0).astype(jnp.float32)
    onehot = (labels_ref[0:1, :] == wanted).astype(jnp.float32).T.astype(jnp.bfloat16)
    picks = jnp.dot(
        jnp.concatenate([onehot] * 3, axis=1),
        jnp.concatenate(thirds(sparse), axis=0),
        preferred_element_type=jnp.float32,
    )
    for j in range(OWN):
        out_ref[:, j * COUNT : (j + 1) * COUNT, :] = picks[
            :, j * POINTS : (j + 1) * POINTS
        ].reshape(PEERS, COUNT, POINTS)


def unpack_kernel(back_ref, out_hbm, held, sem):
    chunk = COUNT // CHUNKS
    copies = []
    for i in range(CHUNKS):
        for r in range(i * chunk, (i + 1) * chunk):
            for f in range(0, FIELDS, TILE):
                held[r, f : f + TILE, :] = back_ref[f : f + TILE, r, :]
        span = pl.ds(i * chunk, chunk)
        copies.append(pltpu.make_async_copy(held.at[span], out_hbm.at[span], sem.at[i]))
        copies[-1].start()
    for copy in copies:
        copy.wait()


def on_device(grids, table, coefs):
    f32 = jnp.float32
    messages = pl.pallas_call(
        pack_kernel,
        out_shape=jax.ShapeDtypeStruct((PEERS * MESSAGE, POINTS), f32),
        in_specs=[HBM, HBM, HBM],
        out_specs=VMEM,
        scratch_shapes=[
            pltpu.SMEM(table.shape, table.dtype),
            pltpu.SMEM(coefs.shape, coefs.dtype),
            pltpu.VMEM((COUNT, FIELDS, POINTS), f32),
            pltpu.SemaphoreType.DMA((2,)),
            pltpu.SemaphoreType.DMA((CHUNKS,)),
        ],
        compiler_params=ROOM,
    )(*map(in_hbm, (table, coefs, grids.reshape(COUNT, FIELDS, POINTS))))
    got = exchange(messages.reshape(PEERS, 1, MESSAGE * POINTS))
    partial, labels = pl.pallas_call(
        sum_kernel,
        out_shape=(
            jax.ShapeDtypeStruct((OWN, SUBS, POINTS), f32),
            jax.ShapeDtypeStruct((TILE, PEERS * COUNT), f32),
        ),
        in_specs=[VMEM],
        out_specs=(VMEM, VMEM),
        compiler_params=ROOM,
    )(got.reshape(PEERS * MESSAGE, POINTS))
    every = lax.all_gather(partial, "z")
    picks = pl.pallas_call(
        pick_kernel,
        out_shape=jax.ShapeDtypeStruct((PEERS, ROWS, POINTS), f32),
        in_specs=[VMEM, VMEM],
        out_specs=VMEM,
        compiler_params=ROOM,
    )(every, labels)
    back = exchange(picks).reshape(FIELDS, COUNT, POINTS)
    combined = pl.pallas_call(
        unpack_kernel,
        out_shape=jax.ShapeDtypeStruct((COUNT, FIELDS, POINTS), f32),
        in_specs=[VMEM],
        out_specs=HBM,
        scratch_shapes=[
            pltpu.VMEM((COUNT, FIELDS, POINTS), f32),
            pltpu.SemaphoreType.DMA((CHUNKS,)),
        ],
        compiler_params=ROOM,
    )(back)
    return combined.reshape(grids.shape)


def solution(mesh):
    parts = Mesh(mesh.devices.reshape(Y, Z, CORES, -1), ("y", "z", "core", "dom"))
    grp = ("y", "z", "core")
    return jax.shard_map(
        on_device,
        mesh=parts,
        in_specs=(P(grp, None, None, "dom"), P(grp, None), P(grp)),
        out_specs=P(grp, None, None, "dom"),
        check_vma=False,
    )
```

```python
import jax
import jax.numpy as jnp
from jax import lax
from jax.experimental import pallas as pl
from jax.experimental.pallas import tpu as pltpu
from jax.sharding import PartitionSpec as P

SUBS = 64
Y, Z, CORES = 8, 4, 2
PLANES = [[(y * Z + z) * CORES + c for y in range(Y) for c in range(CORES)] for z in range(Z)]


def couples(turn):
    near, wrapped = [(0, 1), (2, 3)], [(1, 2), (0, 3)]
    return [
        [(y * Z + z) * CORES + c for z in couple]
        for y in range(Y)
        for c in range(CORES)
        for couple in (near if turn == c else wrapped)
    ]


PEERS = Y * CORES
COUNT = 16
FIELDS = 64
POINTS = 128
OWN = FIELDS // PEERS
ROWS = OWN * COUNT
MESSAGE = ROWS + 1
TILE = 8
CHUNKS = 4
VMEM = pl.BlockSpec(memory_space=pltpu.VMEM)
ROOM = pltpu.CompilerParams(vmem_limit_bytes=8 << 20)
HBM = pl.BlockSpec(memory_space=pltpu.HBM)


def exchange(value):
    return lax.all_to_all(value, "grp", 0, 0, tiled=True, axis_index_groups=PLANES)


def in_hbm(value):
    return pltpu.with_memory_space_constraint(value, pltpu.HBM)


def thirds(value):
    high = value.astype(jnp.bfloat16)
    rest = value - high.astype(jnp.float32)
    mid = rest.astype(jnp.bfloat16)
    low = (rest - mid.astype(jnp.float32)).astype(jnp.bfloat16)
    return high, mid, low


def pack_kernel(table_hbm, coefs_hbm, grids_hbm, out_ref, table, coefs, grids, known_sem, grids_sem):
    known_copies = [
        pltpu.make_async_copy(table_hbm, table, known_sem.at[0]),
        pltpu.make_async_copy(coefs_hbm, coefs, known_sem.at[1]),
    ]
    chunk = FIELDS // CHUNKS
    spans = [pl.ds(i * chunk, chunk) for i in range(CHUNKS)]
    copies = [
        pltpu.make_async_copy(grids_hbm.at[:, span, :], grids.at[:, span, :], grids_sem.at[i])
        for i, span in enumerate(spans)
    ]
    for copy in known_copies + copies:
        copy.start()
    for copy in known_copies:
        copy.wait()
    slots = table.shape[1]
    lane = lax.broadcasted_iota(jnp.int32, (1, POINTS), 1) % COUNT
    labels = jnp.zeros((1, POINTS), jnp.int32)
    for i in range(COUNT):
        labels = jnp.where(lane == i, table[i // slots, i % slots], labels)
    labels = labels.astype(jnp.float32)
    row = lax.broadcasted_iota(jnp.int32, (COUNT, POINTS), 0)
    weight = jnp.zeros((COUNT, POINTS), jnp.int32)
    for g in range(COUNT // slots):
        weight = jnp.where(row // slots == g, coefs[g], weight)
    weight = weight.astype(jnp.float32)
    for peer in range(PEERS):
        out_ref[peer * MESSAGE + ROWS : (peer + 1) * MESSAGE, :] = labels
    for i, copy in enumerate(copies):
        copy.wait()
        for f in range(i * chunk, (i + 1) * chunk):
            peer, j = divmod(f, OWN)
            at = peer * MESSAGE + j * COUNT
            out_ref[at : at + COUNT, :] = grids[:, f, :] * weight


def in_one_row(rows):
    peer = lax.broadcasted_iota(jnp.int32, rows.shape, 0)
    part = lax.broadcasted_iota(jnp.int32, rows.shape, 1) // COUNT
    per = POINTS // COUNT
    return jnp.concatenate(
        [
            jnp.sum(jnp.where(peer == part + h * per, rows, 0.0), axis=0, keepdims=True)
            for h in range(PEERS // per)
        ],
        axis=1,
    )


def sum_kernel(got_ref, out_ref, labels_ref):
    labels = in_one_row(
        jnp.concatenate(
            [got_ref[(s + 1) * MESSAGE - 1 : (s + 1) * MESSAGE, :] for s in range(PEERS)], axis=0
        )
    )
    wanted = lax.broadcasted_iota(jnp.int32, (SUBS, PEERS * COUNT), 0).astype(jnp.float32)
    onehot = (labels == wanted).astype(jnp.float32).astype(jnp.bfloat16)

    def rows_of(s, j):
        at = s * MESSAGE + j * COUNT
        return got_ref[at : at + COUNT, :]

    data = jnp.concatenate(
        [
            jnp.concatenate([rows_of(s, j) for s in range(PEERS)], axis=0)
            for j in range(OWN)
        ],
        axis=1,
    )
    high, mid, low = (
        jnp.dot(onehot, part, preferred_element_type=jnp.float32) for part in thirds(data)
    )
    total = high + (mid + low)
    for j in range(OWN):
        out_ref[j] = total[:, j * POINTS : (j + 1) * POINTS]
    labels_ref[...] = jnp.broadcast_to(labels, labels_ref.shape)


def pick_kernel(pairs_ref, labels_ref, out_ref):
    sparse = jnp.concatenate([pairs_ref[0, j] + pairs_ref[1, j] for j in range(OWN)], axis=1)
    wanted = lax.broadcasted_iota(jnp.int32, (SUBS, PEERS * COUNT), 0).astype(jnp.float32)
    onehot = (labels_ref[0:1, :] == wanted).astype(jnp.float32).T.astype(jnp.bfloat16)
    picks = jnp.dot(
        jnp.concatenate([onehot] * 3, axis=1),
        jnp.concatenate(thirds(sparse), axis=0),
        preferred_element_type=jnp.float32,
    )
    for j in range(OWN):
        out_ref[:, j * COUNT : (j + 1) * COUNT, :] = picks[
            :, j * POINTS : (j + 1) * POINTS
        ].reshape(PEERS, COUNT, POINTS)


def unpack_kernel(back_ref, out_hbm, held, sem):
    chunk = COUNT // CHUNKS
    copies = []
    for i in range(CHUNKS):
        for r in range(i * chunk, (i + 1) * chunk):
            for f in range(0, FIELDS, TILE):
                held[r, f : f + TILE, :] = back_ref[f : f + TILE, r, :]
        span = pl.ds(i * chunk, chunk)
        copies.append(pltpu.make_async_copy(held.at[span], out_hbm.at[span], sem.at[i]))
        copies[-1].start()
    for copy in copies:
        copy.wait()


def on_device(grids, table, coefs):
    f32 = jnp.float32
    messages = pl.pallas_call(
        pack_kernel,
        out_shape=jax.ShapeDtypeStruct((PEERS * MESSAGE, POINTS), f32),
        in_specs=[HBM, HBM, HBM],
        out_specs=VMEM,
        scratch_shapes=[
            pltpu.SMEM(table.shape, table.dtype),
            pltpu.SMEM(coefs.shape, coefs.dtype),
            pltpu.VMEM((COUNT, FIELDS, POINTS), f32),
            pltpu.SemaphoreType.DMA((2,)),
            pltpu.SemaphoreType.DMA((CHUNKS,)),
        ],
        compiler_params=ROOM,
    )(*map(in_hbm, (table, coefs, grids.reshape(COUNT, FIELDS, POINTS))))
    got = exchange(messages.reshape(PEERS, 1, MESSAGE * POINTS))
    partial, labels = pl.pallas_call(
        sum_kernel,
        out_shape=(
            jax.ShapeDtypeStruct((OWN, SUBS, POINTS), f32),
            jax.ShapeDtypeStruct((TILE, PEERS * COUNT), f32),
        ),
        in_specs=[VMEM],
        out_specs=(VMEM, VMEM),
        compiler_params=ROOM,
    )(got.reshape(PEERS * MESSAGE, POINTS))
    pair = jnp.sum(lax.all_gather(partial, "grp", axis_index_groups=couples(0)), axis=0)
    pairs = lax.all_gather(pair, "grp", axis_index_groups=couples(1))
    picks = pl.pallas_call(
        pick_kernel,
        out_shape=jax.ShapeDtypeStruct((PEERS, ROWS, POINTS), f32),
        in_specs=[VMEM, VMEM],
        out_specs=VMEM,
        compiler_params=ROOM,
    )(pairs, labels)
    back = exchange(picks).reshape(FIELDS, COUNT, POINTS)
    combined = pl.pallas_call(
        unpack_kernel,
        out_shape=jax.ShapeDtypeStruct((COUNT, FIELDS, POINTS), f32),
        in_specs=[VMEM],
        out_specs=HBM,
        scratch_shapes=[
            pltpu.VMEM((COUNT, FIELDS, POINTS), f32),
            pltpu.SemaphoreType.DMA((CHUNKS,)),
        ],
        compiler_params=ROOM,
    )(back)
    return combined.reshape(grids.shape)


def solution(mesh):
    return jax.shard_map(
        on_device,
        mesh=mesh,
        in_specs=(P("grp", None, None, "dom"), P("grp", None), P("grp")),
        out_specs=P("grp", None, None, "dom"),
        check_vma=False,
    )
```

```python
import jax
import jax.numpy as jnp
from jax import lax
from jax.experimental import pallas as pl
from jax.experimental.pallas import tpu as pltpu
from jax.sharding import PartitionSpec as P

SUBS = 64
Y, Z, CORES = 8, 4, 2
PLANES = [[(y * Z + z) * CORES + c for y in range(Y) for c in range(CORES)] for z in range(Z)]


def couples(turn):
    near, wrapped = [(0, 1), (2, 3)], [(1, 2), (0, 3)]
    return [
        [(y * Z + z) * CORES + c for z in couple]
        for y in range(Y)
        for c in range(CORES)
        for couple in (wrapped if turn == c else near)
    ]


PEERS = Y * CORES
COUNT = 16
FIELDS = 64
POINTS = 128
OWN = FIELDS // PEERS
ROWS = OWN * COUNT
MESSAGE = ROWS + 1
TILE = 8
CHUNKS = 4
HALVES = 2
VMEM = pl.BlockSpec(memory_space=pltpu.VMEM)
ROOM = pltpu.CompilerParams(vmem_limit_bytes=8 << 20)
HBM = pl.BlockSpec(memory_space=pltpu.HBM)


def exchange(value):
    return lax.all_to_all(value, "grp", 0, 0, tiled=True, axis_index_groups=PLANES)


def in_hbm(value):
    return pltpu.with_memory_space_constraint(value, pltpu.HBM)


def thirds(value):
    high = value.astype(jnp.bfloat16)
    rest = value - high.astype(jnp.float32)
    mid = rest.astype(jnp.bfloat16)
    low = (rest - mid.astype(jnp.float32)).astype(jnp.bfloat16)
    return high, mid, low


def pack_kernel(table_hbm, coefs_hbm, grids_hbm, out_ref, table, coefs, grids, known_sem, grids_sem):
    known_copies = [
        pltpu.make_async_copy(table_hbm, table, known_sem.at[0]),
        pltpu.make_async_copy(coefs_hbm, coefs, known_sem.at[1]),
    ]
    chunk = FIELDS // CHUNKS
    spans = [pl.ds(i * chunk, chunk) for i in range(CHUNKS)]
    copies = [
        pltpu.make_async_copy(grids_hbm.at[:, span, :], grids.at[:, span, :], grids_sem.at[i])
        for i, span in enumerate(spans)
    ]
    for copy in known_copies + copies:
        copy.start()
    for copy in known_copies:
        copy.wait()
    slots = table.shape[1]
    lane = lax.broadcasted_iota(jnp.int32, (1, POINTS), 1) % COUNT
    labels = jnp.zeros((1, POINTS), jnp.int32)
    for i in range(COUNT):
        labels = jnp.where(lane == i, table[i // slots, i % slots], labels)
    labels = labels.astype(jnp.float32)
    row = lax.broadcasted_iota(jnp.int32, (COUNT, POINTS), 0)
    weight = jnp.zeros((COUNT, POINTS), jnp.int32)
    for g in range(COUNT // slots):
        weight = jnp.where(row // slots == g, coefs[g], weight)
    weight = weight.astype(jnp.float32)
    for peer in range(PEERS):
        out_ref[peer * MESSAGE + ROWS : (peer + 1) * MESSAGE, :] = labels
    for i, copy in enumerate(copies):
        copy.wait()
        for f in range(i * chunk, (i + 1) * chunk):
            peer, j = divmod(f, OWN)
            at = peer * MESSAGE + j * COUNT
            out_ref[at : at + COUNT, :] = grids[:, f, :] * weight


def in_one_row(rows):
    peer = lax.broadcasted_iota(jnp.int32, rows.shape, 0)
    part = lax.broadcasted_iota(jnp.int32, rows.shape, 1) // COUNT
    per = POINTS // COUNT
    return jnp.concatenate(
        [
            jnp.sum(jnp.where(peer == part + h * per, rows, 0.0), axis=0, keepdims=True)
            for h in range(PEERS // per)
        ],
        axis=1,
    )


def sum_kernel(got_ref, out_ref, labels_ref):
    labels = in_one_row(
        jnp.concatenate(
            [got_ref[(s + 1) * MESSAGE - 1 : (s + 1) * MESSAGE, :] for s in range(PEERS)], axis=0
        )
    )
    wanted = lax.broadcasted_iota(jnp.int32, (SUBS, PEERS * COUNT), 0).astype(jnp.float32)
    onehot = (labels == wanted).astype(jnp.float32).astype(jnp.bfloat16)

    def rows_of(s, j):
        at = s * MESSAGE + j * COUNT
        return got_ref[at : at + COUNT, :]

    data = jnp.concatenate(
        [
            jnp.concatenate([rows_of(s, j) for s in range(PEERS)], axis=0)
            for j in range(OWN)
        ],
        axis=1,
    )
    high, mid, low = (
        jnp.dot(onehot, part, preferred_element_type=jnp.float32) for part in thirds(data)
    )
    total = high + (mid + low)
    for j in range(OWN):
        out_ref[j] = total[:, j * POINTS : (j + 1) * POINTS]
    labels_ref[...] = jnp.broadcast_to(labels, labels_ref.shape)


def pick_kernel(pairs_ref, labels_ref, out_ref):
    sparse = jnp.concatenate([pairs_ref[0, j] + pairs_ref[1, j] for j in range(OWN)], axis=1)
    wanted = lax.broadcasted_iota(jnp.int32, (SUBS, PEERS * COUNT), 0).astype(jnp.float32)
    onehot = (labels_ref[0:1, :] == wanted).astype(jnp.float32).T.astype(jnp.bfloat16)
    picks = jnp.dot(
        jnp.concatenate([onehot] * 3, axis=1),
        jnp.concatenate(thirds(sparse), axis=0),
        preferred_element_type=jnp.float32,
    )
    for j in range(OWN):
        out_ref[:, j * COUNT : (j + 1) * COUNT, :] = picks[
            :, j * POINTS : (j + 1) * POINTS
        ].reshape(PEERS, COUNT, POINTS)


def unpack_kernel(back_ref, out_hbm, held, sem):
    direct = COUNT // 2
    chunk = (COUNT - direct) // HALVES
    copies = [
        pltpu.make_async_copy(back_ref.at[:, r, :], out_hbm.at[r], sem.at[r])
        for r in range(direct)
    ]
    for copy in copies:
        copy.start()
    for i in range(HALVES):
        for r in range(i * chunk, (i + 1) * chunk):
            for f in range(0, FIELDS, TILE):
                held[r, f : f + TILE, :] = back_ref[f : f + TILE, direct + r, :]
        copies.append(
            pltpu.make_async_copy(
                held.at[pl.ds(i * chunk, chunk)],
                out_hbm.at[pl.ds(direct + i * chunk, chunk)],
                sem.at[direct + i],
            )
        )
        copies[-1].start()
    for copy in copies:
        copy.wait()


def on_device(grids, table, coefs):
    f32 = jnp.float32
    messages = pl.pallas_call(
        pack_kernel,
        out_shape=jax.ShapeDtypeStruct((PEERS * MESSAGE, POINTS), f32),
        in_specs=[HBM, HBM, HBM],
        out_specs=VMEM,
        scratch_shapes=[
            pltpu.SMEM(table.shape, table.dtype),
            pltpu.SMEM(coefs.shape, coefs.dtype),
            pltpu.VMEM((COUNT, FIELDS, POINTS), f32),
            pltpu.SemaphoreType.DMA((2,)),
            pltpu.SemaphoreType.DMA((CHUNKS,)),
        ],
        compiler_params=ROOM,
    )(*map(in_hbm, (table, coefs, grids.reshape(COUNT, FIELDS, POINTS))))
    got = exchange(messages.reshape(PEERS, 1, MESSAGE * POINTS))
    partial, labels = pl.pallas_call(
        sum_kernel,
        out_shape=(
            jax.ShapeDtypeStruct((OWN, SUBS, POINTS), f32),
            jax.ShapeDtypeStruct((TILE, PEERS * COUNT), f32),
        ),
        in_specs=[VMEM],
        out_specs=(VMEM, VMEM),
        compiler_params=ROOM,
    )(got.reshape(PEERS * MESSAGE, POINTS))
    pair = jnp.sum(lax.all_gather(partial, "grp", axis_index_groups=couples(0)), axis=0)
    pairs = lax.all_gather(pair, "grp", axis_index_groups=couples(1))
    picks = pl.pallas_call(
        pick_kernel,
        out_shape=jax.ShapeDtypeStruct((PEERS, ROWS, POINTS), f32),
        in_specs=[VMEM, VMEM],
        out_specs=VMEM,
        compiler_params=ROOM,
    )(pairs, labels)
    back = exchange(picks).reshape(FIELDS, COUNT, POINTS)
    combined = pl.pallas_call(
        unpack_kernel,
        out_shape=jax.ShapeDtypeStruct((COUNT, FIELDS, POINTS), f32),
        in_specs=[VMEM],
        out_specs=HBM,
        scratch_shapes=[
            pltpu.VMEM((COUNT // 2, FIELDS, POINTS), f32),
            pltpu.SemaphoreType.DMA((COUNT // 2 + HALVES,)),
        ],
        compiler_params=ROOM,
    )(back)
    return combined.reshape(grids.shape)


def solution(mesh):
    return jax.shard_map(
        on_device,
        mesh=mesh,
        in_specs=(P("grp", None, None, "dom"), P("grp", None), P("grp")),
        out_specs=P("grp", None, None, "dom"),
        check_vma=False,
    )
```

```python
import jax
import jax.numpy as jnp
from jax import lax
from jax.experimental import pallas as pl
from jax.experimental.pallas import tpu as pltpu
from jax.sharding import PartitionSpec as P

SUBS = 64
Y, Z, CORES = 8, 4, 2
PLANES = [[(y * Z + z) * CORES + c for y in range(Y) for c in range(CORES)] for z in range(Z)]


def couples(turn):
    near, wrapped = [(0, 1), (2, 3)], [(1, 2), (0, 3)]
    return [
        [(y * Z + z) * CORES + c for z in couple]
        for y in range(Y)
        for c in range(CORES)
        for couple in (near if turn == c else wrapped)
    ]


PEERS = Y * CORES
COUNT = 16
FIELDS = 64
POINTS = 128
OWN = FIELDS // PEERS
ROWS = OWN * COUNT
MESSAGE = ROWS + 1
TILE = 8
CHUNKS = 4
HALVES = 2
VMEM = pl.BlockSpec(memory_space=pltpu.VMEM)
ROOM = pltpu.CompilerParams(vmem_limit_bytes=8 << 20)
HBM = pl.BlockSpec(memory_space=pltpu.HBM)


def exchange(value):
    return lax.all_to_all(value, "grp", 0, 0, tiled=True, axis_index_groups=PLANES)


def in_hbm(value):
    return pltpu.with_memory_space_constraint(value, pltpu.HBM)


def thirds(value):
    high = value.astype(jnp.bfloat16)
    rest = value - high.astype(jnp.float32)
    mid = rest.astype(jnp.bfloat16)
    low = (rest - mid.astype(jnp.float32)).astype(jnp.bfloat16)
    return high, mid, low


def pack_kernel(table_hbm, coefs_hbm, grids_hbm, out_ref, table, coefs, grids, known_sem, grids_sem):
    known_copies = [
        pltpu.make_async_copy(table_hbm, table, known_sem.at[0]),
        pltpu.make_async_copy(coefs_hbm, coefs, known_sem.at[1]),
    ]
    chunk = FIELDS // CHUNKS
    spans = [pl.ds(i * chunk, chunk) for i in range(CHUNKS)]
    copies = [
        pltpu.make_async_copy(grids_hbm.at[:, span, :], grids.at[:, span, :], grids_sem.at[i])
        for i, span in enumerate(spans)
    ]
    for copy in known_copies + copies:
        copy.start()
    for copy in known_copies:
        copy.wait()
    slots = table.shape[1]
    lane = lax.broadcasted_iota(jnp.int32, (1, POINTS), 1) % COUNT
    labels = jnp.zeros((1, POINTS), jnp.int32)
    for i in range(COUNT):
        labels = jnp.where(lane == i, table[i // slots, i % slots], labels)
    labels = labels.astype(jnp.float32)
    row = lax.broadcasted_iota(jnp.int32, (COUNT, POINTS), 0)
    weight = jnp.zeros((COUNT, POINTS), jnp.int32)
    for g in range(COUNT // slots):
        weight = jnp.where(row // slots == g, coefs[g], weight)
    weight = weight.astype(jnp.float32)
    for peer in range(PEERS):
        out_ref[peer * MESSAGE + ROWS : (peer + 1) * MESSAGE, :] = labels
    for i, copy in enumerate(copies):
        copy.wait()
        for f in range(i * chunk, (i + 1) * chunk):
            peer, j = divmod(f, OWN)
            at = peer * MESSAGE + j * COUNT
            out_ref[at : at + COUNT, :] = grids[:, f, :] * weight


def in_one_row(rows):
    peer = lax.broadcasted_iota(jnp.int32, rows.shape, 0)
    part = lax.broadcasted_iota(jnp.int32, rows.shape, 1) // COUNT
    per = POINTS // COUNT
    return jnp.concatenate(
        [
            jnp.sum(jnp.where(peer == part + h * per, rows, 0.0), axis=0, keepdims=True)
            for h in range(PEERS // per)
        ],
        axis=1,
    )


def sum_kernel(got_ref, out_ref, labels_ref):
    labels = in_one_row(
        jnp.concatenate(
            [got_ref[(s + 1) * MESSAGE - 1 : (s + 1) * MESSAGE, :] for s in range(PEERS)], axis=0
        )
    )
    wanted = lax.broadcasted_iota(jnp.int32, (SUBS, PEERS * COUNT), 0).astype(jnp.float32)
    onehot = (labels == wanted).astype(jnp.float32).astype(jnp.bfloat16)

    def rows_of(s, j):
        at = s * MESSAGE + j * COUNT
        return got_ref[at : at + COUNT, :]

    data = jnp.concatenate(
        [
            jnp.concatenate([rows_of(s, j) for s in range(PEERS)], axis=0)
            for j in range(OWN)
        ],
        axis=1,
    )
    high, mid, low = (
        jnp.dot(onehot, part, preferred_element_type=jnp.float32) for part in thirds(data)
    )
    total = high + (mid + low)
    for j in range(OWN):
        out_ref[j] = total[:, j * POINTS : (j + 1) * POINTS]
    labels_ref[...] = jnp.broadcast_to(labels, labels_ref.shape)


def pick_kernel(pairs_ref, labels_ref, out_ref):
    sparse = jnp.concatenate([pairs_ref[0, j] + pairs_ref[1, j] for j in range(OWN)], axis=1)
    wanted = lax.broadcasted_iota(jnp.int32, (SUBS, PEERS * COUNT), 0).astype(jnp.float32)
    onehot = (labels_ref[0:1, :] == wanted).astype(jnp.float32).T.astype(jnp.bfloat16)
    picks = jnp.dot(
        jnp.concatenate([onehot] * 3, axis=1),
        jnp.concatenate(thirds(sparse), axis=0),
        preferred_element_type=jnp.float32,
    )
    for j in range(OWN):
        out_ref[:, j * COUNT : (j + 1) * COUNT, :] = picks[
            :, j * POINTS : (j + 1) * POINTS
        ].reshape(PEERS, COUNT, POINTS)


def unpack_kernel(back_ref, out_hbm, held, sem):
    direct = COUNT // 2
    chunk = (COUNT - direct) // HALVES
    copies = [
        pltpu.make_async_copy(back_ref.at[:, r, :], out_hbm.at[r], sem.at[r])
        for r in range(direct)
    ]
    for copy in copies:
        copy.start()
    for i in range(HALVES):
        for r in range(i * chunk, (i + 1) * chunk):
            for f in range(0, FIELDS, TILE):
                held[r, f : f + TILE, :] = back_ref[f : f + TILE, direct + r, :]
        copies.append(
            pltpu.make_async_copy(
                held.at[pl.ds(i * chunk, chunk)],
                out_hbm.at[pl.ds(direct + i * chunk, chunk)],
                sem.at[direct + i],
            )
        )
        copies[-1].start()
    for copy in copies:
        copy.wait()


def on_device(grids, table, coefs):
    f32 = jnp.float32
    messages = pl.pallas_call(
        pack_kernel,
        out_shape=jax.ShapeDtypeStruct((PEERS * MESSAGE, POINTS), f32),
        in_specs=[HBM, HBM, HBM],
        out_specs=VMEM,
        scratch_shapes=[
            pltpu.SMEM(table.shape, table.dtype),
            pltpu.SMEM(coefs.shape, coefs.dtype),
            pltpu.VMEM((COUNT, FIELDS, POINTS), f32),
            pltpu.SemaphoreType.DMA((2,)),
            pltpu.SemaphoreType.DMA((CHUNKS,)),
        ],
        compiler_params=ROOM,
    )(*map(in_hbm, (table, coefs, grids.reshape(COUNT, FIELDS, POINTS))))
    got = exchange(messages.reshape(PEERS, 1, MESSAGE * POINTS))
    partial, labels = pl.pallas_call(
        sum_kernel,
        out_shape=(
            jax.ShapeDtypeStruct((OWN, SUBS, POINTS), f32),
            jax.ShapeDtypeStruct((TILE, PEERS * COUNT), f32),
        ),
        in_specs=[VMEM],
        out_specs=(VMEM, VMEM),
        compiler_params=ROOM,
    )(got.reshape(PEERS * MESSAGE, POINTS))
    pair = jnp.sum(lax.all_gather(partial, "grp", axis_index_groups=couples(0)), axis=0)
    pairs = lax.all_gather(pair, "grp", axis_index_groups=couples(1))
    picks = pl.pallas_call(
        pick_kernel,
        out_shape=jax.ShapeDtypeStruct((PEERS, ROWS, POINTS), f32),
        in_specs=[VMEM, VMEM],
        out_specs=VMEM,
        compiler_params=ROOM,
    )(pairs, labels)
    back = exchange(picks).reshape(FIELDS, COUNT, POINTS)
    combined = pl.pallas_call(
        unpack_kernel,
        out_shape=jax.ShapeDtypeStruct((COUNT, FIELDS, POINTS), f32),
        in_specs=[VMEM],
        out_specs=HBM,
        scratch_shapes=[
            pltpu.VMEM((COUNT // 2, FIELDS, POINTS), f32),
            pltpu.SemaphoreType.DMA((COUNT // 2 + HALVES,)),
        ],
        compiler_params=ROOM,
    )(back)
    return combined.reshape(grids.shape)


def solution(mesh):
    return jax.shard_map(
        on_device,
        mesh=mesh,
        in_specs=(P("grp", None, None, "dom"), P("grp", None), P("grp")),
        out_specs=P("grp", None, None, "dom"),
        check_vma=False,
    )
```

```python
import jax
import jax.numpy as jnp
from jax import lax
from jax.experimental import pallas as pl
from jax.experimental.pallas import tpu as pltpu
from jax.sharding import PartitionSpec as P

SUBS = 64
Y, Z, CORES = 8, 4, 2
PLANES = [[(y * Z + z) * CORES + c for y in range(Y) for c in range(CORES)] for z in range(Z)]


def couples(turn):
    near, wrapped = [(0, 1), (2, 3)], [(1, 2), (3, 0)]
    return [
        [(y * Z + z) * CORES + c for z in couple]
        for y in range(Y)
        for c in range(CORES)
        for couple in (near if turn == c else wrapped)
    ]


PEERS = Y * CORES
COUNT = 16
FIELDS = 64
POINTS = 128
OWN = FIELDS // PEERS
ROWS = OWN * COUNT
MESSAGE = ROWS + 1
TILE = 8
CHUNKS = 4
VMEM = pl.BlockSpec(memory_space=pltpu.VMEM)
ROOM = pltpu.CompilerParams(vmem_limit_bytes=8 << 20)
HBM = pl.BlockSpec(memory_space=pltpu.HBM)


def exchange(value):
    return lax.all_to_all(value, "grp", 0, 0, tiled=True, axis_index_groups=PLANES)


def in_hbm(value):
    return pltpu.with_memory_space_constraint(value, pltpu.HBM)


def thirds(value):
    high = value.astype(jnp.bfloat16)
    rest = value - high.astype(jnp.float32)
    mid = rest.astype(jnp.bfloat16)
    low = (rest - mid.astype(jnp.float32)).astype(jnp.bfloat16)
    return high, mid, low


def pack_kernel(table_hbm, coefs_hbm, grids_hbm, out_ref, table, coefs, grids, known_sem, grids_sem):
    known_copies = [
        pltpu.make_async_copy(table_hbm, table, known_sem.at[0]),
        pltpu.make_async_copy(coefs_hbm, coefs, known_sem.at[1]),
    ]
    chunk = FIELDS // CHUNKS
    spans = [pl.ds(i * chunk, chunk) for i in range(CHUNKS)]
    copies = [
        pltpu.make_async_copy(grids_hbm.at[:, span, :], grids.at[:, span, :], grids_sem.at[i])
        for i, span in enumerate(spans)
    ]
    for copy in known_copies + copies:
        copy.start()
    for copy in known_copies:
        copy.wait()
    slots = table.shape[1]
    lane = lax.broadcasted_iota(jnp.int32, (1, POINTS), 1) % COUNT
    labels = jnp.zeros((1, POINTS), jnp.int32)
    for i in range(COUNT):
        labels = jnp.where(lane == i, table[i // slots, i % slots], labels)
    labels = labels.astype(jnp.float32)
    row = lax.broadcasted_iota(jnp.int32, (COUNT, POINTS), 0)
    weight = jnp.zeros((COUNT, POINTS), jnp.int32)
    for g in range(COUNT // slots):
        weight = jnp.where(row // slots == g, coefs[g], weight)
    weight = weight.astype(jnp.float32)
    for peer in range(PEERS):
        out_ref[peer * MESSAGE + ROWS : (peer + 1) * MESSAGE, :] = labels
    for i, copy in enumerate(copies):
        copy.wait()
        for f in range(i * chunk, (i + 1) * chunk):
            peer, j = divmod(f, OWN)
            at = peer * MESSAGE + j * COUNT
            out_ref[at : at + COUNT, :] = grids[:, f, :] * weight


def in_one_row(rows):
    peer = lax.broadcasted_iota(jnp.int32, rows.shape, 0)
    part = lax.broadcasted_iota(jnp.int32, rows.shape, 1) // COUNT
    per = POINTS // COUNT
    return jnp.concatenate(
        [
            jnp.sum(jnp.where(peer == part + h * per, rows, 0.0), axis=0, keepdims=True)
            for h in range(PEERS // per)
        ],
        axis=1,
    )


def sum_kernel(got_ref, out_ref, labels_ref):
    labels = in_one_row(
        jnp.concatenate(
            [got_ref[(s + 1) * MESSAGE - 1 : (s + 1) * MESSAGE, :] for s in range(PEERS)], axis=0
        )
    )
    wanted = lax.broadcasted_iota(jnp.int32, (SUBS, PEERS * COUNT), 0).astype(jnp.float32)
    onehot = (labels == wanted).astype(jnp.float32).astype(jnp.bfloat16)

    def rows_of(s, j):
        at = s * MESSAGE + j * COUNT
        return got_ref[at : at + COUNT, :]

    data = jnp.concatenate(
        [
            jnp.concatenate([rows_of(s, j) for s in range(PEERS)], axis=0)
            for j in range(OWN)
        ],
        axis=1,
    )
    high, mid, low = (
        jnp.dot(onehot, part, preferred_element_type=jnp.float32) for part in thirds(data)
    )
    total = high + (mid + low)
    for j in range(OWN):
        out_ref[j] = total[:, j * POINTS : (j + 1) * POINTS]
    labels_ref[...] = jnp.broadcast_to(labels, labels_ref.shape)


def pick_kernel(pairs_ref, labels_ref, out_ref):
    sparse = jnp.concatenate([pairs_ref[0, j] + pairs_ref[1, j] for j in range(OWN)], axis=1)
    wanted = lax.broadcasted_iota(jnp.int32, (SUBS, PEERS * COUNT), 0).astype(jnp.float32)
    onehot = (labels_ref[0:1, :] == wanted).astype(jnp.float32).T.astype(jnp.bfloat16)
    picks = jnp.dot(
        jnp.concatenate([onehot] * 3, axis=1),
        jnp.concatenate(thirds(sparse), axis=0),
        preferred_element_type=jnp.float32,
    )
    for j in range(OWN):
        out_ref[:, j * COUNT : (j + 1) * COUNT, :] = picks[
            :, j * POINTS : (j + 1) * POINTS
        ].reshape(PEERS, COUNT, POINTS)


def unpack_kernel(back_ref, out_hbm, held, sem):
    chunk = COUNT // CHUNKS
    copies = []
    for i in range(CHUNKS):
        for r in range(i * chunk, (i + 1) * chunk):
            for f in range(0, FIELDS, TILE):
                held[r, f : f + TILE, :] = back_ref[f : f + TILE, r, :]
        span = pl.ds(i * chunk, chunk)
        copies.append(pltpu.make_async_copy(held.at[span], out_hbm.at[span], sem.at[i]))
        copies[-1].start()
    for copy in copies:
        copy.wait()


def on_device(grids, table, coefs):
    f32 = jnp.float32
    messages = pl.pallas_call(
        pack_kernel,
        out_shape=jax.ShapeDtypeStruct((PEERS * MESSAGE, POINTS), f32),
        in_specs=[HBM, HBM, HBM],
        out_specs=VMEM,
        scratch_shapes=[
            pltpu.SMEM(table.shape, table.dtype),
            pltpu.SMEM(coefs.shape, coefs.dtype),
            pltpu.VMEM((COUNT, FIELDS, POINTS), f32),
            pltpu.SemaphoreType.DMA((2,)),
            pltpu.SemaphoreType.DMA((CHUNKS,)),
        ],
        compiler_params=ROOM,
    )(*map(in_hbm, (table, coefs, grids.reshape(COUNT, FIELDS, POINTS))))
    got = exchange(messages.reshape(PEERS, 1, MESSAGE * POINTS))
    partial, labels = pl.pallas_call(
        sum_kernel,
        out_shape=(
            jax.ShapeDtypeStruct((OWN, SUBS, POINTS), f32),
            jax.ShapeDtypeStruct((TILE, PEERS * COUNT), f32),
        ),
        in_specs=[VMEM],
        out_specs=(VMEM, VMEM),
        compiler_params=ROOM,
    )(got.reshape(PEERS * MESSAGE, POINTS))
    pair = jnp.sum(lax.all_gather(partial, "grp", axis_index_groups=couples(0)), axis=0)
    pairs = lax.all_gather(pair, "grp", axis_index_groups=couples(1))
    picks = pl.pallas_call(
        pick_kernel,
        out_shape=jax.ShapeDtypeStruct((PEERS, ROWS, POINTS), f32),
        in_specs=[VMEM, VMEM],
        out_specs=VMEM,
        compiler_params=ROOM,
    )(pairs, labels)
    back = exchange(picks).reshape(FIELDS, COUNT, POINTS)
    combined = pl.pallas_call(
        unpack_kernel,
        out_shape=jax.ShapeDtypeStruct((COUNT, FIELDS, POINTS), f32),
        in_specs=[VMEM],
        out_specs=HBM,
        scratch_shapes=[
            pltpu.VMEM((COUNT, FIELDS, POINTS), f32),
            pltpu.SemaphoreType.DMA((CHUNKS,)),
        ],
        compiler_params=ROOM,
    )(back)
    return combined.reshape(grids.shape)


def solution(mesh):
    return jax.shard_map(
        on_device,
        mesh=mesh,
        in_specs=(P("grp", None, None, "dom"), P("grp", None), P("grp")),
        out_specs=P("grp", None, None, "dom"),
        check_vma=False,
    )
```

```python
import jax
import jax.numpy as jnp
from jax import lax
from jax.experimental import pallas as pl
from jax.experimental.pallas import tpu as pltpu
from jax.sharding import PartitionSpec as P

SUBS = 64
Y, Z, CORES = 8, 4, 2
PLANES = [[(y * Z + z) * CORES + c for y in range(Y) for c in range(CORES)] for z in range(Z)]


def couples(turn):
    near, wrapped = [(0, 1), (2, 3)], [(1, 2), (0, 3)]
    return [
        [(y * Z + z) * CORES + c for z in couple]
        for y in range(Y)
        for c in range(CORES)
        for couple in (near if turn == c else wrapped)
    ]


PEERS = Y * CORES
COUNT = 16
FIELDS = 64
POINTS = 128
OWN = FIELDS // PEERS
ROWS = OWN * COUNT
MESSAGE = ROWS + 1
TILE = 8
CHUNKS = 2
VMEM = pl.BlockSpec(memory_space=pltpu.VMEM)
ROOM = pltpu.CompilerParams(vmem_limit_bytes=8 << 20)
HBM = pl.BlockSpec(memory_space=pltpu.HBM)


def exchange(value):
    return lax.all_to_all(value, "grp", 0, 0, tiled=True, axis_index_groups=PLANES)


def in_hbm(value):
    return pltpu.with_memory_space_constraint(value, pltpu.HBM)


def thirds(value):
    high = value.astype(jnp.bfloat16)
    rest = value - high.astype(jnp.float32)
    mid = rest.astype(jnp.bfloat16)
    low = (rest - mid.astype(jnp.float32)).astype(jnp.bfloat16)
    return high, mid, low


def pack_kernel(table_hbm, coefs_hbm, grids_hbm, out_ref, table, coefs, grids, known_sem, grids_sem):
    known_copies = [
        pltpu.make_async_copy(table_hbm, table, known_sem.at[0]),
        pltpu.make_async_copy(coefs_hbm, coefs, known_sem.at[1]),
    ]
    chunk = FIELDS // CHUNKS
    spans = [pl.ds(i * chunk, chunk) for i in range(CHUNKS)]
    copies = [
        pltpu.make_async_copy(grids_hbm.at[:, span, :], grids.at[:, span, :], grids_sem.at[i])
        for i, span in enumerate(spans)
    ]
    for copy in known_copies + copies:
        copy.start()
    for copy in known_copies:
        copy.wait()
    slots = table.shape[1]
    lane = lax.broadcasted_iota(jnp.int32, (1, POINTS), 1) % COUNT
    labels = jnp.zeros((1, POINTS), jnp.int32)
    for i in range(COUNT):
        labels = jnp.where(lane == i, table[i // slots, i % slots], labels)
    labels = labels.astype(jnp.float32)
    row = lax.broadcasted_iota(jnp.int32, (COUNT, POINTS), 0)
    weight = jnp.zeros((COUNT, POINTS), jnp.int32)
    for g in range(COUNT // slots):
        weight = jnp.where(row // slots == g, coefs[g], weight)
    weight = weight.astype(jnp.float32)
    for peer in range(PEERS):
        out_ref[peer * MESSAGE + ROWS : (peer + 1) * MESSAGE, :] = labels
    for i, copy in enumerate(copies):
        copy.wait()
        for f in range(i * chunk, (i + 1) * chunk):
            peer, j = divmod(f, OWN)
            at = peer * MESSAGE + j * COUNT
            out_ref[at : at + COUNT, :] = grids[:, f, :] * weight


def in_one_row(rows):
    peer = lax.broadcasted_iota(jnp.int32, rows.shape, 0)
    part = lax.broadcasted_iota(jnp.int32, rows.shape, 1) // COUNT
    per = POINTS // COUNT
    return jnp.concatenate(
        [
            jnp.sum(jnp.where(peer == part + h * per, rows, 0.0), axis=0, keepdims=True)
            for h in range(PEERS // per)
        ],
        axis=1,
    )


def sum_kernel(got_ref, out_ref, labels_ref):
    labels = in_one_row(
        jnp.concatenate(
            [got_ref[(s + 1) * MESSAGE - 1 : (s + 1) * MESSAGE, :] for s in range(PEERS)], axis=0
        )
    )
    wanted = lax.broadcasted_iota(jnp.int32, (SUBS, PEERS * COUNT), 0).astype(jnp.float32)
    onehot = (labels == wanted).astype(jnp.float32).astype(jnp.bfloat16)

    def rows_of(s, j):
        at = s * MESSAGE + j * COUNT
        return got_ref[at : at + COUNT, :]

    data = jnp.concatenate(
        [
            jnp.concatenate([rows_of(s, j) for s in range(PEERS)], axis=0)
            for j in range(OWN)
        ],
        axis=1,
    )
    high, mid, low = (
        jnp.dot(onehot, part, preferred_element_type=jnp.float32) for part in thirds(data)
    )
    total = high + (mid + low)
    for j in range(OWN):
        out_ref[j] = total[:, j * POINTS : (j + 1) * POINTS]
    labels_ref[...] = jnp.broadcast_to(labels, labels_ref.shape)


def pick_kernel(pairs_ref, labels_ref, out_ref):
    sparse = jnp.concatenate([pairs_ref[0, j] + pairs_ref[1, j] for j in range(OWN)], axis=1)
    wanted = lax.broadcasted_iota(jnp.int32, (SUBS, PEERS * COUNT), 0).astype(jnp.float32)
    onehot = (labels_ref[0:1, :] == wanted).astype(jnp.float32).T.astype(jnp.bfloat16)
    picks = jnp.dot(
        jnp.concatenate([onehot] * 3, axis=1),
        jnp.concatenate(thirds(sparse), axis=0),
        preferred_element_type=jnp.float32,
    )
    for j in range(OWN):
        out_ref[:, j * COUNT : (j + 1) * COUNT, :] = picks[
            :, j * POINTS : (j + 1) * POINTS
        ].reshape(PEERS, COUNT, POINTS)


def unpack_kernel(back_ref, out_hbm, held, sem):
    chunk = COUNT // CHUNKS
    copies = []
    for i in range(CHUNKS):
        for r in range(i * chunk, (i + 1) * chunk):
            for f in range(0, FIELDS, TILE):
                held[r, f : f + TILE, :] = back_ref[f : f + TILE, r, :]
        span = pl.ds(i * chunk, chunk)
        copies.append(pltpu.make_async_copy(held.at[span], out_hbm.at[span], sem.at[i]))
        copies[-1].start()
    for copy in copies:
        copy.wait()


def on_device(grids, table, coefs):
    f32 = jnp.float32
    messages = pl.pallas_call(
        pack_kernel,
        out_shape=jax.ShapeDtypeStruct((PEERS * MESSAGE, POINTS), f32),
        in_specs=[HBM, HBM, HBM],
        out_specs=VMEM,
        scratch_shapes=[
            pltpu.SMEM(table.shape, table.dtype),
            pltpu.SMEM(coefs.shape, coefs.dtype),
            pltpu.VMEM((COUNT, FIELDS, POINTS), f32),
            pltpu.SemaphoreType.DMA((2,)),
            pltpu.SemaphoreType.DMA((CHUNKS,)),
        ],
        compiler_params=ROOM,
    )(*map(in_hbm, (table, coefs, grids.reshape(COUNT, FIELDS, POINTS))))
    got = exchange(messages.reshape(PEERS, 1, MESSAGE * POINTS))
    partial, labels = pl.pallas_call(
        sum_kernel,
        out_shape=(
            jax.ShapeDtypeStruct((OWN, SUBS, POINTS), f32),
            jax.ShapeDtypeStruct((TILE, PEERS * COUNT), f32),
        ),
        in_specs=[VMEM],
        out_specs=(VMEM, VMEM),
        compiler_params=ROOM,
    )(got.reshape(PEERS * MESSAGE, POINTS))
    pair = jnp.sum(lax.all_gather(partial, "grp", axis_index_groups=couples(0)), axis=0)
    pairs = lax.all_gather(pair, "grp", axis_index_groups=couples(1))
    picks = pl.pallas_call(
        pick_kernel,
        out_shape=jax.ShapeDtypeStruct((PEERS, ROWS, POINTS), f32),
        in_specs=[VMEM, VMEM],
        out_specs=VMEM,
        compiler_params=ROOM,
    )(pairs, labels)
    back = exchange(picks).reshape(FIELDS, COUNT, POINTS)
    combined = pl.pallas_call(
        unpack_kernel,
        out_shape=jax.ShapeDtypeStruct((COUNT, FIELDS, POINTS), f32),
        in_specs=[VMEM],
        out_specs=HBM,
        scratch_shapes=[
            pltpu.VMEM((COUNT, FIELDS, POINTS), f32),
            pltpu.SemaphoreType.DMA((CHUNKS,)),
        ],
        compiler_params=ROOM,
    )(back)
    return combined.reshape(grids.shape)


def solution(mesh):
    return jax.shard_map(
        on_device,
        mesh=mesh,
        in_specs=(P("grp", None, None, "dom"), P("grp", None), P("grp")),
        out_specs=P("grp", None, None, "dom"),
        check_vma=False,
    )
```
